32 devices in a mesh: row: 4 (over z), col: 8 (over y, x, core).
Axes of the slice: x: 2, y: 2, z: 4, core: 2. Of those that a mesh axis runs over, the one named last changes fastest.
Arguments:
- s_slab: bfloat16 [128, 262144], P(None, ('row', 'col')), may hold values from -4 to 4
- p_blocks: bfloat16 [4, 8, 64, 128, 128], P('row', 'col'), may hold values from -0.5 to 0.5
- p_index: int32 [4, 8, 2, 64], P('row', 'col'), may hold values from -1 to 2047, as said below
Outputs:
- purified: bfloat16 [128, 262144], P(None, ('row', 'col'))
The draws below stay inside these ranges and needn't reach their ends.
Inputs may be any that keep to these rules, and one draw needn't show every extreme that they name: `p_index`: the slot on device (r, c) holds blocks whose block column lies in r * 512 to (r + 1) * 512 - 1 and whose block row k has (k // 64) % 8 == c; no block appears twice; live slots come first in each device's list and both entries of a slot are -1 or both are live; some device has all 64 slots live in every draw.
All inputs are finite; a program needn't handle non-finite values.
Results may differ from the reference program's by a relative error of at most 0.0034.
Values may be sent and summed in bfloat16 or wider, within the bound.
No kernel may reach another device: no remote copies, remote signals or barrier semaphores. Data moves between devices by JAX's collectives and lax.ppermute only.
A program may use at most 192 MiB of HBM per device.

```python
import jax
import jax.numpy as jnp
from jax import lax

BLK = 128
NB = 2048
NPB = 64
SPAN = 512
N_ROW = 4
N_COL = 8


def draw_p_index(key, part):
    key = jax.random.fold_in(key, 11)
    devices = N_ROW * N_COL
    kspan = NB // N_COL
    jspan = NB // N_ROW
    per_piece = NB // devices
    key_count, key_full, key_perm = jax.random.split(key, 3)
    counts = jax.random.randint(key_count, (devices,), NPB // 8, NPB - NPB // 8 + 1)
    fullest = jax.random.randint(key_full, (), 0, devices)
    counts = jnp.where(jnp.arange(devices) == fullest, NPB, counts)
    keys = jax.random.split(key_perm, devices)

    def one_device(device_key, device, count):
        order = jax.random.permutation(device_key, kspan * jspan)[:NPB].astype(jnp.int32)
        inner = order // jspan
        outer = order % jspan
        row_here = device // N_COL
        col_here = device % N_COL
        block_rows = (inner // per_piece * N_COL + col_here) * per_piece + inner % per_piece
        block_cols = row_here * jspan + outer
        live = jnp.arange(NPB) < count
        return jnp.stack([jnp.where(live, block_rows, -1), jnp.where(live, block_cols, -1)]).astype(jnp.int32)
    result = jax.vmap(one_device)(keys, jnp.arange(devices, dtype=jnp.int32), counts)
    return result.reshape(N_ROW, N_COL, 2, NPB)


def level_of(rng, extent, cuts, least, largest):
    level = 1.0
    for position, blocks in cuts:
        heights = jax.random.uniform(jax.random.fold_in(jax.random.fold_in(rng, 6), position), (blocks,), jnp.float32, least / len(cuts), largest / len(cuts))
        level = level * jnp.repeat(jnp.exp(heights), extent[position] // blocks).reshape((-1,) + (1,) * (len(extent) - 1 - position))
    return level


def centred(stream_key, dims, width, bound, pieces=(), kind=jnp.bfloat16):
    values = jax.random.normal(stream_key, dims, jnp.float32) * width
    if len(pieces) > 0:
        values = level_of(stream_key, dims, pieces, -0.22, 0.18) * values
    return jnp.clip(values, min=-bound, max=bound).astype(kind)


def setup_inputs(seed: int = 0) -> dict:
    splits = jax.random.split(jax.random.key(seed), 4)
    return {
        "s_slab": centred(splits[0], (BLK, NB * BLK), 0.5, 4.0, ((1, 32),)),
        "p_blocks": centred(splits[1], (N_ROW, N_COL, NPB, BLK, BLK), (BLK * max(1, N_COL * NPB // (2 * (NB // N_ROW)))) ** -0.5, 0.5, ((0, 4), (1, 8))),
        "p_index": draw_p_index(jax.random.fold_in(splits[3], 71), 0),
    }


def reference(s_slab, p_blocks, p_index):
    panels = s_slab.reshape(BLK, NB, BLK)

    def per_row(row_here):
        blocks = p_blocks[row_here]
        index = p_index[row_here]

        def per_device(total, item):
            stored, coords = item
            block_rows = jnp.clip(coords[0], 0, NB - 1).astype(jnp.int32)
            local_cols = jnp.where(coords[1] >= 0, coords[1] - row_here * SPAN, SPAN).astype(jnp.int32)
            taken = jnp.take(panels, block_rows, axis=1)
            product = jnp.einsum("agk,gkb->gab", taken.astype(jnp.float32), stored.astype(jnp.float32))
            contribution = jax.ops.segment_sum(product, local_cols, num_segments=SPAN)
            rounded = lax.optimization_barrier(contribution.astype(jnp.bfloat16))
            return total + rounded.astype(jnp.float32), None

        start = jnp.zeros((SPAN, BLK, BLK), jnp.float32)
        total, unused = lax.scan(per_device, start, (blocks, index))
        return total

    cube = lax.map(per_row, jnp.arange(N_ROW, dtype=jnp.int32))
    cube = cube.reshape(NB, BLK, BLK).transpose(1, 0, 2).reshape(BLK, NB * BLK)
    return (3.0 * s_slab.astype(jnp.float32) - 2.0 * cube).astype(jnp.bfloat16)
```

```python
import jax
import jax.numpy as jnp
from jax import lax
from jax.experimental import pallas as pl
from jax.experimental.pallas import tpu as pltpu
from jax.sharding import PartitionSpec as P

CAP_ROW = 24
CAP_COL = 16
PARTS = 2
VMEM_LIMIT = 60 * 1024 * 1024


def smem():
    return pl.BlockSpec(memory_space=pltpu.SMEM)


def anywhere():
    return pl.BlockSpec(memory_space=pl.ANY)


def pairs(n, t):
    return [(i, i ^ t) for i in range(n)]


def ask_kernel(n_row, n_col, per_piece, cap, base, index, *refs):
    asks, place, most = refs[:n_row], refs[n_row], refs[n_row + 1]
    mark, table, count, start = refs[n_row + 2 :]
    slots = index.shape[1]
    row = lax.axis_index("row")
    for t in range(n_row):
        count[t] = 0
        start[t] = base[t]

    def where(s):
        k = jnp.maximum(index[0, s], 0)
        return lax.div(k, per_piece * n_col), lax.rem(k, per_piece)

    def clear(s, carry):
        owner, panel = where(s)
        mark[owner * per_piece + panel] = -1
        return carry

    lax.fori_loop(0, slots, clear, 0, unroll=8)

    def step(s, carry):
        owner, panel = where(s)
        spot = owner * per_piece + panel
        t = owner ^ row
        seen = mark[spot]
        fresh = (index[0, s] >= 0) & (seen < 0)
        held = count[t]
        at = jnp.where(seen < 0, held, seen)

        @pl.when(fresh)
        def _():
            mark[spot] = held
            table[t, held] = panel
            count[t] = held + 1

        limit = jnp.where(t == 0, table.shape[1], cap)
        place[0, s] = start[t] + jnp.minimum(at, limit - 1)
        return carry + jnp.where(index[0, s] >= 0, 1, 0)

    live = lax.fori_loop(0, slots, step, 0)
    largest = 0
    for t in range(n_row):
        asks[t][0, 0] = count[t]
        if t > 0:
            largest = jnp.maximum(largest, count[t])

        def copy(i, carry):
            asks[t][0, 1 + i] = table[t, i]
            return carry

        lax.fori_loop(0, count[t], copy, 0)
    most[0, 0] = largest
    most[0, 1] = live


def plan_kernel(n_col, per_piece, cap, base, trash, index, lists, place, most, mark, count, start):
    slots = index.shape[1]
    col = lax.axis_index("col")
    for t in range(n_col):
        count[t] = 0
        start[t] = base[t]

    def where(s):
        j = jnp.maximum(index[1, s], 0)
        piece = lax.div(j, per_piece)
        return lax.rem(piece, n_col), j - piece * per_piece

    def clear(s, carry):
        owner, panel = where(s)
        mark[owner * per_piece + panel] = -1
        return carry

    lax.fori_loop(0, slots, clear, 0, unroll=8)

    def step(s, carry):
        owner, panel = where(s)
        spot = owner * per_piece + panel
        t = owner ^ col
        seen = mark[spot]
        alive = index[1, s] >= 0
        fresh = alive & (seen < 0)
        held = count[t]
        at = jnp.where(seen < 0, held, seen)

        @pl.when(fresh)
        def _():
            mark[spot] = held
            lists[owner, 1 + held] = panel
            count[t] = held + 1

        limit = jnp.where(t == 0, min(per_piece, slots), cap)
        spot_out = start[t] + jnp.minimum(at, limit - 1)
        place[0, s] = jnp.where(alive, spot_out, trash)
        place[1, s] = jnp.where(fresh, 1, 0)
        return carry

    lax.fori_loop(0, slots, step, 0)
    largest = 0
    for t in range(n_col):
        lists[col ^ t, 0] = count[t]
        if t > 0:
            largest = jnp.maximum(largest, count[t])
    most[0, 0] = largest


def pack_kernel(blk, *refs):
    n_row = (len(refs) - 1) // 2
    asks, slab, packs = refs[:n_row], refs[n_row], refs[n_row + 1 :]
    for ask, pack in zip(asks, packs):

        def copy(i, carry):
            at = pl.multiple_of(ask[0, 1 + i] * blk, blk)
            pack[i] = slab[:, pl.ds(at, blk)]
            return carry

        lax.fori_loop(0, jnp.minimum(ask[0, 0], pack.shape[0]), copy, 0)


def product_kernel(n_row, n_col, base_in, base_out, group, place_in, place_out, most, lists, stored, *refs):
    panels, sums = refs[:n_row], refs[n_row : n_row + n_col]
    held, total, sems = refs[n_row + n_col :]
    copies = [
        pltpu.make_async_copy(panel, held.at[pl.ds(base_in[t], panel.shape[0])], sems.at[t])
        for t, panel in enumerate(panels)
    ]
    for copy in copies:
        copy.start()
    for copy in copies:
        copy.wait()
    live = most[0, 1]

    def step(g, carry):
        products = []
        for u in range(group):
            s = g * group + u
            products.append(
                jnp.dot(held[place_in[0, s]], stored[s], preferred_element_type=jnp.float32)
            )
        for u in range(group):
            s = g * group + u
            o = place_out[0, s]
            before = jnp.where(place_out[1, s] == 1, 0.0, total[o])
            total[o] = before + products[u]
        return carry

    lax.fori_loop(0, lax.div(live + group - 1, group), step, 0)
    col = lax.axis_index("col")
    for t in range(n_col):

        def store(i, carry):
            sums[t][i] = total[base_out[t] + i].astype(jnp.bfloat16)
            return carry

        lax.fori_loop(0, jnp.minimum(lists[col ^ t, 0], sums[t].shape[0]), store, 0)


def combine_kernel(n_col, blk, lists, slab, *refs):
    sums, out, total = refs[:n_col], refs[-2], refs[-1]
    col = lax.axis_index("col")
    pieces = out.shape[1] // blk
    total[...] = jnp.zeros_like(total)
    for t in range(n_col):
        source = col ^ t

        def add(i, carry):
            at = lists[source, 1 + i]
            total[at] += sums[t][i].astype(jnp.float32)
            return carry

        lax.fori_loop(0, jnp.minimum(lists[source, 0], sums[t].shape[0]), add, 0)
    for i in range(pieces):
        here = pl.ds(i * blk, blk)
        out[:, here] = (3.0 * slab[:, here].astype(jnp.float32) - 2.0 * total[i]).astype(out.dtype)


def dense(s_slab, p_blocks, p_index):
    blk = s_slab.shape[0]
    per_piece = s_slab.shape[1] // blk
    n_row = lax.axis_size("row")
    n_col = lax.axis_size("col")
    span = n_col * per_piece
    gathered = lax.all_gather(s_slab, "row", axis=1, tiled=True)
    panels = gathered.reshape(blk, n_row * per_piece, blk)
    block_rows = p_index[0, 0, 0]
    block_cols = p_index[0, 0, 1]
    local_rows = jnp.clip(
        block_rows // per_piece // n_col * per_piece + block_rows % per_piece,
        0,
        n_row * per_piece - 1,
    )
    local_cols = jnp.where(block_cols >= 0, block_cols - lax.axis_index("row") * span, span)
    taken = jnp.take(panels, local_rows, axis=1)
    product = jnp.einsum("agk,gkb->gab", taken, p_blocks[0, 0], preferred_element_type=jnp.float32)
    term = jax.ops.segment_sum(product, local_cols, num_segments=span)
    cube = lax.psum_scatter(term.astype(jnp.bfloat16), "col", scatter_dimension=0, tiled=True)
    cube = cube.astype(jnp.float32).transpose(1, 0, 2).reshape(blk, per_piece * blk)
    return (3.0 * s_slab.astype(jnp.float32) - 2.0 * cube).astype(jnp.bfloat16)


def body(s_slab, p_blocks, p_index):
    blk = s_slab.shape[0]
    per_piece = s_slab.shape[1] // blk
    n_row = lax.axis_size("row")
    n_col = lax.axis_size("col")
    slots = p_blocks.shape[2]
    stored = p_blocks[0, 0]
    index = p_index[0, 0]
    full = min(per_piece, slots)
    cap_row = min(CAP_ROW, full)
    cap_col = min(CAP_COL, full)
    wide = -(-(1 + full) // 128) * 128
    caps_in = [full] + [cap_row] * (n_row - 1)
    caps_out = [full] + [cap_col] * (n_col - 1)
    base_in = [sum(caps_in[:t]) for t in range(n_row)]
    base_out = [sum(caps_out[:t]) for t in range(n_col)]
    trash = sum(caps_out)
    parts = PARTS if blk % (16 * PARTS) == 0 else 1
    rows = blk // parts
    group = 4 if slots % 4 == 0 else 1
    params = pltpu.CompilerParams(vmem_limit_bytes=VMEM_LIMIT)
    table = jax.ShapeDtypeStruct((1, wide), jnp.int32)

    asked = pl.pallas_call(
        lambda *refs: ask_kernel(n_row, n_col, per_piece, cap_row, base_in, *refs),
        out_shape=[table] * n_row + [jax.ShapeDtypeStruct((1, slots), jnp.int32), table],
        in_specs=[smem()],
        out_specs=[smem()] * (n_row + 2),
        scratch_shapes=[
            pltpu.SMEM((n_row * per_piece,), jnp.int32),
            pltpu.SMEM((n_row, full), jnp.int32),
            pltpu.SMEM((n_row,), jnp.int32),
            pltpu.SMEM((n_row,), jnp.int32),
        ],
        name="ask",
    )(index)
    asks, place_in, most_in = asked[:n_row], asked[n_row], asked[n_row + 1]
    asks = [asks[0]] + [lax.ppermute(asks[t], "row", pairs(n_row, t)) for t in range(1, n_row)]

    lists, place_out, most_out = pl.pallas_call(
        lambda *refs: plan_kernel(n_col, per_piece, cap_col, base_out, trash, *refs),
        out_shape=[
            jax.ShapeDtypeStruct((n_col, wide), jnp.int32),
            jax.ShapeDtypeStruct((2, slots), jnp.int32),
            table,
        ],
        in_specs=[smem()],
        out_specs=[smem()] * 3,
        scratch_shapes=[
            pltpu.SMEM((n_col * per_piece,), jnp.int32),
            pltpu.SMEM((n_col,), jnp.int32),
            pltpu.SMEM((n_col,), jnp.int32),
        ],
        name="plan",
    )(index)
    arriving = lax.all_to_all(lists, "col", 0, 0, tiled=True)

    packed = []
    for part in range(parts):
        packed.append(
            pl.pallas_call(
                lambda *refs: pack_kernel(blk, *refs),
                grid=(1,),
                out_shape=[jax.ShapeDtypeStruct((cap, rows, blk), jnp.bfloat16) for cap in caps_in],
                in_specs=[smem()] * n_row
                + [pl.BlockSpec((rows, s_slab.shape[1]), lambda i, part=part: (part, 0))],
                out_specs=[pl.BlockSpec((cap, rows, blk), lambda i: (0, 0, 0)) for cap in caps_in],
                compiler_params=params,
                cost_estimate=pl.CostEstimate(
                    flops=0, bytes_accessed=2 * s_slab.size * 2 // parts, transcendentals=0
                ),
                name="pack",
            )(*asks, s_slab)
        )
    fetched = [
        [packed[part][0]]
        + [lax.ppermute(packed[part][t], "row", pairs(n_row, t)) for t in range(1, n_row)]
        for part in range(parts)
    ]
    sums = []
    for part in range(parts):
        done = pl.pallas_call(
            lambda *refs: product_kernel(n_row, n_col, base_in, base_out, group, *refs),
            out_shape=[jax.ShapeDtypeStruct((cap, rows, blk), jnp.bfloat16) for cap in caps_out],
            in_specs=[smem()] * 4
            + [pl.BlockSpec(memory_space=pltpu.VMEM)]
            + [anywhere()] * n_row,
            out_specs=[pl.BlockSpec(memory_space=pltpu.VMEM)] * n_col,
            scratch_shapes=[
                pltpu.VMEM((sum(caps_in), rows, blk), jnp.bfloat16),
                pltpu.VMEM((trash + 1, rows, blk), jnp.float32),
                pltpu.SemaphoreType.DMA((n_row,)),
            ],
            compiler_params=params,
            cost_estimate=pl.CostEstimate(
                flops=2 * slots * rows * blk * blk,
                bytes_accessed=2 * blk * blk * slots + 2 * rows * blk * (sum(caps_in) + trash),
                transcendentals=0,
            ),
            name="product",
        )(place_in, place_out, most_in, lists, stored, *fetched[part])
        sums.append(
            [done[0]] + [lax.ppermute(done[t], "col", pairs(n_col, t)) for t in range(1, n_col)]
        )

    def combine(part, before):
        extra = [] if before is None else [before]
        return pl.pallas_call(
            lambda *refs: combine_kernel(n_col, blk, *refs),
            grid=(1,),
            out_shape=jax.ShapeDtypeStruct(s_slab.shape, s_slab.dtype),
            in_specs=[smem()]
            + [pl.BlockSpec((rows, s_slab.shape[1]), lambda i: (part, 0))]
            + [pl.BlockSpec((cap, rows, blk), lambda i: (0, 0, 0)) for cap in caps_out]
            + [anywhere()] * len(extra),
            out_specs=pl.BlockSpec((rows, s_slab.shape[1]), lambda i: (part, 0)),
            scratch_shapes=[pltpu.VMEM((per_piece, rows, blk), jnp.float32)],
            input_output_aliases={2 + n_col: 0} if extra else {},
            compiler_params=params,
            cost_estimate=pl.CostEstimate(
                flops=4 * s_slab.size // parts,
                bytes_accessed=4 * s_slab.size // parts + 2 * rows * blk * trash,
                transcendentals=0,
            ),
            name="combine",
        )(arriving, s_slab, *sums[part], *extra)

    result = None
    for part in range(parts - 1):
        result = combine(part, result)
    if cap_row == full and cap_col == full:
        return combine(parts - 1, result)
    over = jnp.maximum(most_in[0, 0] - cap_row, most_out[0, 0] - cap_col)
    over = lax.pmax(over, ("row", "col"))
    return lax.cond(
        over > 0,
        lambda: dense(s_slab, p_blocks, p_index),
        lambda: combine(parts - 1, result),
    )


def solution(mesh):
    placed = (
        P(None, ("row", "col")),
        P("row", "col", None, None, None),
        P("row", "col", None, None),
    )
    return jax.shard_map(
        body, mesh=mesh, in_specs=placed, out_specs=P(None, ("row", "col")), check_vma=False
    )
```

```python
import jax
import jax.numpy as jnp
from jax import lax
from jax.experimental import pallas as pl
from jax.experimental.pallas import tpu as pltpu
from jax.sharding import PartitionSpec as P

CAP_ROW = 24
CAP_COL = 16
PARTS = 2
VMEM_LIMIT = 60 * 1024 * 1024


def smem():
    return pl.BlockSpec(memory_space=pltpu.SMEM)


def anywhere():
    return pl.BlockSpec(memory_space=pl.ANY)


def one(shape, at=None):
    at = (0,) * len(shape) if at is None else at
    return pl.BlockSpec(shape, lambda i: at)


def number(index, per_piece, owner_of, n_owner, cap, wide):
    slots = index.shape[1]
    f32 = jnp.float32
    lane = lax.broadcasted_iota(jnp.int32, (slots, slots), 1)
    sub = lax.broadcasted_iota(jnp.int32, (slots, slots), 0)
    key_r = index.astype(f32)
    key_c = jnp.sum(jnp.where(lane == sub, key_r, 0.0), axis=1, keepdims=True)
    index_c = key_c.astype(jnp.int32)

    def split(values):
        return owner_of(jnp.maximum(values, 0)).astype(f32), lax.rem(jnp.maximum(values, 0), per_piece).astype(f32)

    owner_r, _ = split(index)
    owner_c, local_c = split(index_c)
    same = jnp.where(key_c == key_r, 1.0, 0.0)
    before = jnp.where(lane < sub, 1.0, 0.0)
    after = jnp.where(sub < lane, 1.0, 0.0)
    kin = jnp.where(owner_c == owner_r, 1.0, 0.0)
    first_c = jnp.where(jnp.sum(same * before, axis=1, keepdims=True) == 0.0, 1.0, 0.0)
    first_c = jnp.where(key_c >= 0.0, first_c, 0.0)
    first_r = jnp.where(jnp.sum(same * after, axis=0, keepdims=True) == 0.0, 1.0, 0.0)
    first_r = jnp.where(key_r >= 0.0, first_r, 0.0)
    rank_c = jnp.sum(kin * before * first_r, axis=1, keepdims=True)
    at_r = jnp.sum(same * (first_c * rank_c), axis=0, keepdims=True)
    place = owner_r * cap + jnp.minimum(at_r, cap - 1.0)
    wide_lane = lax.broadcasted_iota(jnp.int32, (slots, wide), 1).astype(f32)
    spot = jnp.where(wide_lane == rank_c + 1.0, local_c, 0.0) + jnp.where(wide_lane == 0.0, 1.0, 0.0)
    rows = []
    for owner in range(n_owner):
        mine = first_c * jnp.where(owner_c == float(owner), 1.0, 0.0)
        rows.append(jnp.sum(spot * mine, axis=0, keepdims=True))
    return place, first_r, rows


def ask_kernel(n_row, n_col, per_piece, cap_row, cap_col, index, asks, lists, places):
    wide = asks.shape[1]
    k, j = index[0, 0, 0:1, :], index[0, 0, 1:2, :]
    place_in, _, ask_rows = number(
        k, per_piece, lambda v: lax.div(v, per_piece * n_col), n_row, cap_row, wide
    )
    place_out, first, list_rows = number(
        j, per_piece, lambda v: lax.rem(lax.div(v, per_piece), n_col), n_col, cap_col, wide
    )
    excess = jnp.full((1, 1), -1.0, jnp.float32)
    for cap, rows in ((cap_row, ask_rows), (cap_col, list_rows)):
        for row in rows:
            excess = jnp.maximum(excess, row[:, 0:1] - float(cap))
    lane = lax.broadcasted_iota(jnp.int32, (1, wide), 1)
    for i, row in enumerate(ask_rows):
        asks[i : i + 1, :] = jnp.where(lane == wide - 1, excess, row).astype(jnp.int32)
    for i, row in enumerate(list_rows):
        lists[i : i + 1, :] = row.astype(jnp.int32)
    alive = jnp.where(j >= 0, 1.0, 0.0)
    places[0:1, :] = place_in.astype(jnp.int32)
    places[1:2, :] = jnp.where(j >= 0, place_out, float(n_col * cap_col)).astype(jnp.int32)
    places[2:3, :] = first.astype(jnp.int32)
    live = jnp.sum(alive, axis=1, keepdims=True)
    places[3:4, :] = jnp.broadcast_to(live, j.shape).astype(jnp.int32)


def pack_kernel(blk, asks, slab, packs):
    n_row, cap = packs.shape[:2]
    for t in range(n_row):

        def copy(i, carry):
            at = pl.multiple_of(asks[t, 1 + i] * blk, blk)
            packs[t, i] = slab[:, pl.ds(at, blk)]
            return carry

        lax.fori_loop(0, jnp.minimum(asks[t, 0], cap), copy, 0)


def product_kernel(group, places, lists, stored, panels, sums, total):
    n_col, cap = sums.shape[:2]
    slots = places.shape[1]
    live = places[3, 0]

    def step(g, carry):
        products = []
        for u in range(group):
            s = g * group + u
            products.append(
                jnp.dot(panels[places[0, s]], stored[s], preferred_element_type=jnp.float32)
            )
        for u in range(group):
            s = g * group + u
            o = places[1, s]
            total[o] = jnp.where(places[2, s] == 1, 0.0, total[o]) + products[u]
        return carry

    lax.fori_loop(0, lax.div(live + group - 1, group), step, 0)
    for t in range(n_col):

        def store(i, carry):
            sums[t, i] = total[t * cap + i].astype(jnp.bfloat16)
            return carry

        lax.fori_loop(0, jnp.minimum(lists[t, 0], cap), store, 0)


def combine_kernel(blk, lists, slab, sums, *refs):
    out, total = refs[-2], refs[-1]
    n_col, cap = sums.shape[:2]
    total[...] = jnp.zeros_like(total)
    for t in range(n_col):

        def add(i, carry):
            total[lists[t, 1 + i]] += sums[t, i].astype(jnp.float32)
            return carry

        lax.fori_loop(0, jnp.minimum(lists[t, 0], cap), add, 0)
    for i in range(out.shape[1] // blk):
        here = pl.ds(i * blk, blk)
        out[:, here] = (3.0 * slab[:, here].astype(jnp.float32) - 2.0 * total[i]).astype(out.dtype)


def dense(s_slab, p_blocks, p_index):
    blk = s_slab.shape[0]
    per_piece = s_slab.shape[1] // blk
    n_row = lax.axis_size("row")
    n_col = lax.axis_size("col")
    span = n_col * per_piece
    gathered = lax.all_gather(s_slab, "row", axis=1, tiled=True)
    panels = gathered.reshape(blk, n_row * per_piece, blk)
    block_rows = p_index[0, 0, 0]
    block_cols = p_index[0, 0, 1]
    local_rows = jnp.clip(
        block_rows // per_piece // n_col * per_piece + block_rows % per_piece,
        0,
        n_row * per_piece - 1,
    )
    local_cols = jnp.where(block_cols >= 0, block_cols - lax.axis_index("row") * span, span)
    taken = jnp.take(panels, local_rows, axis=1)
    product = jnp.einsum("agk,gkb->gab", taken, p_blocks[0, 0], preferred_element_type=jnp.float32)
    term = jax.ops.segment_sum(product, local_cols, num_segments=span)
    cube = lax.psum_scatter(term.astype(jnp.bfloat16), "col", scatter_dimension=0, tiled=True)
    cube = cube.astype(jnp.float32).transpose(1, 0, 2).reshape(blk, per_piece * blk)
    return (3.0 * s_slab.astype(jnp.float32) - 2.0 * cube).astype(jnp.bfloat16)


def body(s_slab, p_blocks, p_index):
    blk = s_slab.shape[0]
    per_piece = s_slab.shape[1] // blk
    n_row = lax.axis_size("row")
    n_col = lax.axis_size("col")
    slots = p_blocks.shape[2]
    stored = p_blocks[0, 0]
    full = min(per_piece, slots)
    cap_row = min(CAP_ROW, full)
    cap_col = min(CAP_COL, full)
    wide = -(-(2 + full) // 128) * 128
    parts = PARTS if blk % (16 * PARTS) == 0 else 1
    rows = blk // parts
    group = 4 if slots % 4 == 0 else 1
    params = pltpu.CompilerParams(vmem_limit_bytes=VMEM_LIMIT)

    asks, lists, places = pl.pallas_call(
        lambda *refs: ask_kernel(n_row, n_col, per_piece, cap_row, cap_col, *refs),
        out_shape=[
            jax.ShapeDtypeStruct((n_row, wide), jnp.int32),
            jax.ShapeDtypeStruct((n_col, wide), jnp.int32),
            jax.ShapeDtypeStruct((4, slots), jnp.int32),
        ],
        compiler_params=params,
        name="ask",
    )(p_index)
    asked = lax.all_to_all(asks, "row", 0, 0, tiled=True)

    packed = [
        pl.pallas_call(
            lambda *refs: pack_kernel(blk, *refs),
            grid=(1,),
            out_shape=jax.ShapeDtypeStruct((n_row, cap_row, rows, blk), jnp.bfloat16),
            in_specs=[smem(), one((rows, s_slab.shape[1]), (part, 0))],
            out_specs=one((n_row, cap_row, rows, blk)),
            compiler_params=params,
            cost_estimate=pl.CostEstimate(
                flops=0, bytes_accessed=4 * s_slab.size // parts, transcendentals=0
            ),
            name="pack",
        )(asked, s_slab)
        for part in range(parts)
    ]
    fetched = [lax.all_to_all(part, "row", 0, 0, tiled=True) for part in packed]

    worst = jnp.max(asked[:, wide - 1])
    told = jnp.where(jnp.arange(wide)[None] == wide - 1, worst, lists)
    told = lax.all_to_all(told, "col", 0, 0, tiled=True)

    sums = []
    for part in range(parts):
        done = pl.pallas_call(
            lambda *refs: product_kernel(group, *refs),
            grid=(1,),
            out_shape=jax.ShapeDtypeStruct((n_col, cap_col, rows, blk), jnp.bfloat16),
            in_specs=[smem()] * 2
            + [one(stored.shape), one((n_row * cap_row, rows, blk))],
            out_specs=one((n_col, cap_col, rows, blk)),
            scratch_shapes=[pltpu.VMEM((n_col * cap_col + 1, rows, blk), jnp.float32)],
            compiler_params=params,
            cost_estimate=pl.CostEstimate(
                flops=2 * slots * rows * blk * blk,
                bytes_accessed=2 * blk * blk * slots
                + 2 * rows * blk * (n_row * cap_row + n_col * cap_col),
                transcendentals=0,
            ),
            name="product",
        )(places, lists, stored, fetched[part].reshape(n_row * cap_row, rows, blk))
        sums.append(lax.all_to_all(done, "col", 0, 0, tiled=True))

    def combine(part, before):
        extra = [] if before is None else [before]
        return pl.pallas_call(
            lambda *refs: combine_kernel(blk, *refs),
            grid=(1,),
            out_shape=jax.ShapeDtypeStruct(s_slab.shape, s_slab.dtype),
            in_specs=[
                smem(),
                one((rows, s_slab.shape[1]), (part, 0)),
                one((n_col, cap_col, rows, blk)),
            ]
            + [anywhere()] * len(extra),
            out_specs=one((rows, s_slab.shape[1]), (part, 0)),
            scratch_shapes=[pltpu.VMEM((per_piece, rows, blk), jnp.float32)],
            input_output_aliases={3: 0} if extra else {},
            compiler_params=params,
            cost_estimate=pl.CostEstimate(
                flops=4 * s_slab.size // parts,
                bytes_accessed=4 * s_slab.size // parts + 2 * rows * blk * n_col * cap_col,
                transcendentals=0,
            ),
            name="combine",
        )(told, s_slab, sums[part], *extra)

    result = None
    for part in range(parts - 1):
        result = combine(part, result)
    if cap_row == full and cap_col == full:
        return combine(parts - 1, result)
    return lax.cond(
        jnp.max(told[:, wide - 1]) > 0,
        lambda: dense(s_slab, p_blocks, p_index),
        lambda: combine(parts - 1, result),
    )


def solution(mesh):
    placed = (
        P(None, ("row", "col")),
        P("row", "col", None, None, None),
        P("row", "col", None, None),
    )
    return jax.shard_map(
        body, mesh=mesh, in_specs=placed, out_specs=P(None, ("row", "col")), check_vma=False
    )
```

```python
import jax
import jax.numpy as jnp
from jax import lax
from jax.experimental import pallas as pl
from jax.experimental.pallas import tpu as pltpu
from jax.sharding import PartitionSpec as P

LEVELS = ((28, 16, 14), (28, 18, 14), (28, 20, 16), (32, 24, 20))
PARTS = (64, 32, 32)
SHIFT = 1024
VMEM_LIMIT = 60 * 1024 * 1024


def smem():
    return pl.BlockSpec(memory_space=pltpu.SMEM)


def anywhere():
    return pl.BlockSpec(memory_space=pl.ANY)


def one(shape, at=None):
    at = (0,) * len(shape) if at is None else at
    return pl.BlockSpec(shape, lambda i: at)


def pairs(n, t):
    return [(i, i ^ t) for i in range(n)]


def number(index, per_piece, owner_of, n_owner, wide):
    slots = index.shape[1]
    f32 = jnp.float32
    lane = lax.broadcasted_iota(jnp.int32, (slots, slots), 1)
    sub = lax.broadcasted_iota(jnp.int32, (slots, slots), 0)
    key_r = index.astype(f32)
    key_c = jnp.sum(jnp.where(lane == sub, key_r, 0.0), axis=1, keepdims=True)
    index_c = jnp.maximum(key_c.astype(jnp.int32), 0)
    owner_r = owner_of(jnp.maximum(index, 0)).astype(f32)
    owner_c = owner_of(index_c).astype(f32)
    local_c = lax.rem(index_c, per_piece).astype(f32)
    same = jnp.where(key_c == key_r, 1.0, 0.0)
    before = jnp.where(lane < sub, 1.0, 0.0)
    after = jnp.where(sub < lane, 1.0, 0.0)
    kin = jnp.where(owner_c == owner_r, 1.0, 0.0)
    first_c = jnp.where(jnp.sum(same * before, axis=1, keepdims=True) == 0.0, 1.0, 0.0)
    first_c = jnp.where(key_c >= 0.0, first_c, 0.0)
    first_r = jnp.where(jnp.sum(same * after, axis=0, keepdims=True) == 0.0, 1.0, 0.0)
    first_r = jnp.where(key_r >= 0.0, first_r, 0.0)
    rank_c = jnp.sum(kin * before * first_r, axis=1, keepdims=True)
    rank_r = jnp.sum(same * (first_c * rank_c), axis=0, keepdims=True)
    lanes = lax.broadcasted_iota(jnp.int32, (slots, wide), 1).astype(f32)
    spot = jnp.where(lanes == rank_c + 1.0, local_c, 0.0) + jnp.where(lanes == 0.0, 1.0, 0.0)
    rows = []
    for owner in range(n_owner):
        mine = first_c * jnp.where(owner_c == float(owner), 1.0, 0.0)
        rows.append(jnp.sum(spot * mine, axis=0, keepdims=True))
    return owner_r.astype(jnp.int32), rank_r.astype(jnp.int32), first_r, rows


def ask_kernel(n_row, n_col, per_piece, levels, index, line, places):
    wide = line.shape[1]
    k, j = index[0, 0, 0:1, :], index[0, 0, 1:2, :]
    from_r, from_rank, _, asks = number(
        k, per_piece, lambda v: lax.div(v, per_piece * n_col), n_row, wide
    )
    to_r, to_rank, first, lists = number(
        j, per_piece, lambda v: lax.rem(lax.div(v, per_piece), n_col), n_col, wide
    )
    row = lax.axis_index("row")
    need = jnp.zeros((1, 1), jnp.float32)
    for near, far, col in levels:
        over = jnp.zeros((1, 1), jnp.float32)
        for owner, ask in enumerate(asks):
            cap = jnp.where((owner ^ row) <= 1, float(near), float(far))
            over = jnp.maximum(over, jnp.where(ask[:, 0:1] > cap, 1.0, 0.0))
        for item in lists:
            over = jnp.maximum(over, jnp.where(item[:, 0:1] > float(col), 1.0, 0.0))
        need = need + over
    lane = lax.broadcasted_iota(jnp.int32, (1, wide), 1)
    told = jnp.concatenate(lists, axis=0) * float(SHIFT)
    for owner, ask in enumerate(asks):
        values = jnp.where(lane == wide - 1, need, ask + told)
        line[owner * n_col : (owner + 1) * n_col, :] = values.astype(jnp.int32)
    alive = jnp.where(j >= 0, 1.0, 0.0)
    live = jnp.sum(alive, axis=1, keepdims=True)
    places[0:1, :] = from_r ^ row
    places[1:2, :] = from_rank
    places[2:3, :] = to_r
    places[3:4, :] = to_rank
    places[4:5, :] = first.astype(jnp.int32)
    places[5:6, :] = jnp.broadcast_to(live, j.shape).astype(jnp.int32)


def fetch(copies):
    for copy in copies:
        copy.start()
    for copy in copies:
        copy.wait()


def pack_kernel(n_row, n_col, blk, heard, slab, *refs):
    packs, (asks, sems) = refs[:n_row], refs[n_row:]
    row, col = lax.axis_index("row"), lax.axis_index("col")
    fetch(
        [
            pltpu.make_async_copy(heard.at[(row ^ t) * n_col + col], asks.at[t], sems.at[t])
            for t in range(n_row)
        ]
    )
    for t in range(n_row):

        def copy(i, carry):
            at = pl.multiple_of((asks[t, 0, 1 + i] & (SHIFT - 1)) * blk, blk)
            packs[t][i] = slab[:, pl.ds(at, blk)]
            return carry

        lax.fori_loop(0, asks[t, 0, 0] & (SHIFT - 1), copy, 0)


def product_kernel(n_row, base, group, places, stored, *refs):
    panels = refs[:n_row]
    sums, held, total, sems = refs[n_row:]
    n_col, cap = sums.shape[:2]
    fetch(
        [
            pltpu.make_async_copy(panel, held.at[pl.ds(base[t], panel.shape[0])], sems.at[t])
            for t, panel in enumerate(panels)
        ]
    )
    live = places[5, 0]

    def start(t):
        at = jnp.int32(base[0])
        for i in range(1, n_row):
            at = jnp.where(t == i, base[i], at)
        return at

    def step(g, carry):
        products = []
        for u in range(group):
            s = g * group + u
            here = start(places[0, s]) + places[1, s]
            products.append(jnp.dot(held[here], stored[s], preferred_element_type=jnp.float32))
        for u in range(group):
            s = g * group + u
            o = jnp.where(s < live, places[2, s] * cap + places[3, s], n_col * cap)
            total[o] = jnp.where(places[4, s] == 1, 0.0, total[o]) + products[u]
        return carry

    lax.fori_loop(0, lax.div(live + group - 1, group), step, 0)

    def store(s, carry):
        @pl.when(places[4, s] == 1)
        def _():
            to, at = places[2, s], places[3, s]
            sums[to, at] = total[to * cap + at].astype(jnp.bfloat16)

        return carry

    lax.fori_loop(0, live, store, 0)


def combine_kernel(n_row, n_col, blk, heard, slab, sums, *refs):
    out, total, lists, sems = refs[-4:]
    row = lax.axis_index("row")
    copies = [
        pltpu.make_async_copy(heard.at[row * n_col + t], lists.at[t], sems.at[t])
        for t in range(n_col)
    ]
    for copy in copies:
        copy.start()
    total[...] = jnp.zeros_like(total)
    for copy in copies:
        copy.wait()
    for t in range(n_col):

        def add(i, carry):
            total[lists[t, 0, 1 + i] >> 10] += sums[t, i].astype(jnp.float32)
            return carry

        lax.fori_loop(0, lists[t, 0, 0] >> 10, add, 0)
    for i in range(out.shape[1] // blk):
        here = pl.ds(i * blk, blk)
        out[:, here] = (3.0 * slab[:, here].astype(jnp.float32) - 2.0 * total[i]).astype(out.dtype)


def exchange(heard, places, s_slab, stored, caps_in, cap, parts):
    blk = s_slab.shape[0]
    width = s_slab.shape[1]
    n_row = lax.axis_size("row")
    n_col = lax.axis_size("col")
    slots = stored.shape[0]
    group = 4 if slots % 4 == 0 else 1
    base = [sum(caps_in[:t]) for t in range(n_row)]
    params = pltpu.CompilerParams(vmem_limit_bytes=VMEM_LIMIT)
    firsts = [sum(parts[:i]) for i in range(len(parts))]
    result = None
    packed = [
        pl.pallas_call(
            lambda *refs: pack_kernel(n_row, n_col, blk, *refs),
            grid=(1,),
            out_shape=[jax.ShapeDtypeStruct((c, rows, blk), jnp.bfloat16) for c in caps_in],
            in_specs=[anywhere(), one((rows, width), (first // rows, 0))],
            out_specs=[one((c, rows, blk)) for c in caps_in],
            scratch_shapes=[
                pltpu.SMEM((n_row,) + heard.shape[1:], jnp.int32),
                pltpu.SemaphoreType.DMA((n_row,)),
            ],
            compiler_params=params,
            cost_estimate=pl.CostEstimate(
                flops=0, bytes_accessed=4 * rows * width, transcendentals=0
            ),
            name="pack",
        )(heard, s_slab)
        for first, rows in zip(firsts, parts)
    ]
    for first, rows, packs in zip(firsts, parts, packed):
        panels = [packs[0]] + [
            lax.ppermute(packs[t], "row", pairs(n_row, t)) for t in range(1, n_row)
        ]
        sums = pl.pallas_call(
            lambda *refs: product_kernel(n_row, base, group, *refs),
            grid=(1,),
            out_shape=jax.ShapeDtypeStruct((n_col, cap, rows, blk), jnp.bfloat16),
            in_specs=[smem(), one(stored.shape)] + [anywhere()] * n_row,
            out_specs=one((n_col, cap, rows, blk)),
            scratch_shapes=[
                pltpu.VMEM((sum(caps_in), rows, blk), jnp.bfloat16),
                pltpu.VMEM((n_col * cap + 1, rows, blk), jnp.float32),
                pltpu.SemaphoreType.DMA((n_row,)),
            ],
            compiler_params=params,
            cost_estimate=pl.CostEstimate(
                flops=2 * slots * rows * blk * blk,
                bytes_accessed=2 * blk * blk * slots + 2 * rows * blk * (sum(caps_in) + n_col * cap),
                transcendentals=0,
            ),
            name="product",
        )(places, stored, *panels)
        sums = lax.all_to_all(sums, "col", 0, 0, tiled=True)
        extra = [] if result is None else [result]
        result = pl.pallas_call(
            lambda *refs: combine_kernel(n_row, n_col, blk, *refs),
            grid=(1,),
            out_shape=jax.ShapeDtypeStruct(s_slab.shape, s_slab.dtype),
            in_specs=[
                anywhere(),
                one((rows, width), (first // rows, 0)),
                one((n_col, cap, rows, blk)),
            ]
            + [anywhere()] * len(extra),
            out_specs=one((rows, width), (first // rows, 0)),
            scratch_shapes=[
                pltpu.VMEM((width // blk, rows, blk), jnp.float32),
                pltpu.SMEM((n_col,) + heard.shape[1:], jnp.int32),
                pltpu.SemaphoreType.DMA((n_col,)),
            ],
            input_output_aliases={3: 0} if extra else {},
            compiler_params=params,
            cost_estimate=pl.CostEstimate(
                flops=4 * rows * width,
                bytes_accessed=4 * rows * width + 2 * rows * blk * n_col * cap,
                transcendentals=0,
            ),
            name="combine",
        )(heard, s_slab, sums, *extra)
    return result


def body(s_slab, p_blocks, p_index):
    blk = s_slab.shape[0]
    per_piece = s_slab.shape[1] // blk
    n_row = lax.axis_size("row")
    n_col = lax.axis_size("col")
    slots = p_blocks.shape[2]
    stored = p_blocks[0, 0]
    full = min(per_piece, slots)
    wide = -(-(2 + full) // 128) * 128
    parts = PARTS if sum(PARTS) == blk else (blk,)
    levels = [level for level in LEVELS if max(level) < full]
    levels.append((full, full, full))

    line, places = pl.pallas_call(
        lambda *refs: ask_kernel(n_row, n_col, per_piece, levels[:-1], *refs),
        out_shape=[
            jax.ShapeDtypeStruct((n_row * n_col, wide), jnp.int32),
            jax.ShapeDtypeStruct((6, slots), jnp.int32),
        ],
        name="ask",
    )(p_index)
    heard = lax.all_to_all(line, ("row", "col"), 0, 0, tiled=True)
    lines = heard.reshape(n_row * n_col, 1, wide)

    def run(level):
        near, far, cap = level
        caps_in = [near, near] + [far] * (n_row - 2)
        return lambda: exchange(lines, places, s_slab, stored, caps_in, cap, parts)

    if len(levels) == 1:
        return run(levels[0])()
    return lax.switch(jnp.max(heard[:, wide - 1]), [run(level) for level in levels])


def solution(mesh):
    placed = (
        P(None, ("row", "col")),
        P("row", "col", None, None, None),
        P("row", "col", None, None),
    )
    return jax.shard_map(
        body, mesh=mesh, in_specs=placed, out_specs=P(None, ("row", "col")), check_vma=False
    )
```

```python
import jax
import jax.numpy as jnp
from jax import lax
from jax.experimental import pallas as pl
from jax.experimental.pallas import tpu as pltpu
from jax.sharding import PartitionSpec as P

LEVELS = ((28, 16, 14), (28, 18, 14), (28, 20, 16), (32, 24, 20))
PARTS = (32, 32, 32, 32)
SHIFT = 1024
COST = 1 << 16


def smem():
    return pl.BlockSpec(memory_space=pltpu.SMEM)


def anywhere():
    return pl.BlockSpec(memory_space=pl.ANY)


def vmem():
    return pl.BlockSpec(memory_space=pltpu.VMEM)


def pairs(n, t):
    return [(i, i ^ t) for i in range(n)]


def number(index, per_piece, owner_of, n_owner, wide):
    slots = index.shape[1]
    f32 = jnp.float32
    lane = lax.broadcasted_iota(jnp.int32, (slots, slots), 1)
    sub = lax.broadcasted_iota(jnp.int32, (slots, slots), 0)
    key_r = index.astype(f32)
    key_c = jnp.sum(jnp.where(lane == sub, key_r, 0.0), axis=1, keepdims=True)
    index_c = jnp.maximum(key_c.astype(jnp.int32), 0)
    owner_r = owner_of(jnp.maximum(index, 0)).astype(f32)
    owner_c = owner_of(index_c).astype(f32)
    local_c = lax.rem(index_c, per_piece).astype(f32)
    same = jnp.where(key_c == key_r, 1.0, 0.0)
    before = jnp.where(lane < sub, 1.0, 0.0)
    after = jnp.where(sub < lane, 1.0, 0.0)
    kin = jnp.where(owner_c == owner_r, 1.0, 0.0)
    first_c = jnp.where(jnp.sum(same * before, axis=1, keepdims=True) == 0.0, 1.0, 0.0)
    first_c = jnp.where(key_c >= 0.0, first_c, 0.0)
    first_r = jnp.where(jnp.sum(same * after, axis=0, keepdims=True) == 0.0, 1.0, 0.0)
    first_r = jnp.where(key_r >= 0.0, first_r, 0.0)
    rank_c = jnp.sum(kin * before * first_r, axis=1, keepdims=True)
    rank_r = jnp.sum(same * (first_c * rank_c), axis=0, keepdims=True)
    lanes = lax.broadcasted_iota(jnp.int32, (slots, wide), 1).astype(f32)
    spot = jnp.where(lanes == rank_c + 1.0, local_c, 0.0) + jnp.where(lanes == 0.0, 1.0, 0.0)
    rows = []
    for owner in range(n_owner):
        mine = first_c * jnp.where(owner_c == float(owner), 1.0, 0.0)
        rows.append(jnp.sum(spot * mine, axis=0, keepdims=True))
    return owner_r.astype(jnp.int32), rank_r.astype(jnp.int32), first_r, rows


def ask_kernel(n_row, n_col, per_piece, levels, index, line, places):
    wide = line.shape[1]
    k, j = index[0, 0, 0:1, :], index[0, 0, 1:2, :]
    from_r, from_rank, _, asks = number(
        k, per_piece, lambda v: lax.div(v, per_piece * n_col), n_row, wide
    )
    to_r, to_rank, first, lists = number(
        j, per_piece, lambda v: lax.rem(lax.div(v, per_piece), n_col), n_col, wide
    )
    row = lax.axis_index("row")
    need = jnp.zeros((1, 1), jnp.float32)
    for near, far, col in levels:
        over = jnp.zeros((1, 1), jnp.float32)
        for owner, ask in enumerate(asks):
            cap = jnp.where((owner ^ row) <= 1, float(near), float(far))
            over = jnp.maximum(over, jnp.where(ask[:, 0:1] > cap, 1.0, 0.0))
        for item in lists:
            over = jnp.maximum(over, jnp.where(item[:, 0:1] > float(col), 1.0, 0.0))
        need = need + over
    lane = lax.broadcasted_iota(jnp.int32, (1, wide), 1)
    told = jnp.concatenate(lists, axis=0) * float(SHIFT)
    for owner, ask in enumerate(asks):
        values = jnp.where(lane == wide - 1, need, ask + told)
        line[owner * n_col : (owner + 1) * n_col, :] = values.astype(jnp.int32)
    alive = jnp.where(j >= 0, 1.0, 0.0)
    live = jnp.sum(alive, axis=1, keepdims=True)
    places[0:1, :] = from_r ^ row
    places[1:2, :] = from_rank
    places[2:3, :] = to_r
    places[3:4, :] = to_rank
    places[4:5, :] = first.astype(jnp.int32)
    places[5:6, :] = jnp.broadcast_to(live, j.shape).astype(jnp.int32)


def fetch(copies):
    for copy in copies:
        copy.start()
    for copy in copies:
        copy.wait()


def pack_kernel(n_row, n_col, blk, spans, heard, slab, *refs):
    packs, (asks, sems) = refs[: n_row * len(spans)], refs[n_row * len(spans) :]
    row, col = lax.axis_index("row"), lax.axis_index("col")
    fetch(
        [
            pltpu.make_async_copy(heard.at[(row ^ t) * n_col + col], asks.at[t], sems.at[t])
            for t in range(n_row)
        ]
    )
    for p, (first, rows) in enumerate(spans):
        for t in range(n_row):
            pack = packs[p * n_row + t]

            def copy(i, carry):
                at = pl.multiple_of((asks[t, 0, 1 + i] & (SHIFT - 1)) * blk, blk)
                pack[i] = slab[first : first + rows, pl.ds(at, blk)]
                return carry

            lax.fori_loop(0, asks[t, 0, 0] & (SHIFT - 1), copy, 0)


def product_kernel(n_row, base, group, places, stored, *refs):
    panels = refs[:n_row]
    sums, held, total = refs[-3:]
    n_col, cap = sums.shape[:2]
    for t, panel in enumerate(panels):
        held[base[t] : base[t] + panel.shape[0]] = panel[...]
    live = places[5, 0]

    def start(t):
        at = jnp.int32(base[0])
        for i in range(1, n_row):
            at = jnp.where(t == i, base[i], at)
        return at

    def step(g, carry):
        products = []
        for u in range(group):
            s = g * group + u
            here = start(places[0, s]) + places[1, s]
            products.append(jnp.dot(held[here], stored[s], preferred_element_type=jnp.float32))
        for u in range(group):
            s = g * group + u
            o = jnp.where(s < live, places[2, s] * cap + places[3, s], n_col * cap)
            total[o] = jnp.where(places[4, s] == 1, 0.0, total[o]) + products[u]
        return carry

    lax.fori_loop(0, lax.div(live + group - 1, group), step, 0)
    for t in range(n_col):
        sums[t] = total[t * cap : (t + 1) * cap].astype(jnp.bfloat16)


def combine_kernel(blk, first, chunks, lists, slab, sums, *refs):
    out, total, ready, sems = refs[-4:]
    n_col = sums.shape[0]
    pieces, rows = total.shape[:2]
    for i in range(pieces):
        total[i] = 3.0 * slab[first : first + rows, i * blk : (i + 1) * blk].astype(jnp.float32)
    for t in range(n_col):

        def add(i, carry):
            total[lists[t, 1 + i] >> 10] -= 2.0 * sums[t, i].astype(jnp.float32)
            return carry

        lax.fori_loop(0, lists[t, 0] >> 10, add, 0)
    each = pieces // chunks
    copies = []
    for q in range(chunks):
        for i in range(q * each, (q + 1) * each):
            ready[:, i * blk : (i + 1) * blk] = total[i].astype(ready.dtype)
        here = pl.ds(q * each * blk, each * blk)
        copies.append(
            pltpu.make_async_copy(ready.at[:, here], out.at[pl.ds(first, rows), here], sems.at[q])
        )
        copies[-1].start()
    for copy in copies:
        copy.wait()


def exchange(heard, lists, places, s_slab, stored, caps_in, cap, parts):
    blk = s_slab.shape[0]
    width = s_slab.shape[1]
    n_row = lax.axis_size("row")
    n_col = lax.axis_size("col")
    slots = stored.shape[0]
    pieces = width // blk
    group = 8 if slots % 8 == 0 else 1
    chunks = 4 if pieces % 4 == 0 else 1
    base = [sum(caps_in[:t]) for t in range(n_row)]
    tight = sum(caps_in) <= 2 * slots
    params = pltpu.CompilerParams(vmem_limit_bytes=(16 if tight else 48) * 1024 * 1024)
    cost = pl.CostEstimate(flops=0, bytes_accessed=COST, transcendentals=0)
    spans = [(sum(parts[:i]), rows) for i, rows in enumerate(parts)]

    def pack(some):
        done = pl.pallas_call(
            lambda *refs: pack_kernel(n_row, n_col, blk, some, *refs),
            out_shape=[
                jax.ShapeDtypeStruct((c, rows, blk), jnp.bfloat16)
                for first, rows in some
                for c in caps_in
            ],
            in_specs=[anywhere(), vmem()],
            out_specs=[vmem()] * (n_row * len(some)),
            scratch_shapes=[
                pltpu.SMEM((n_row,) + heard.shape[1:], jnp.int32),
                pltpu.SemaphoreType.DMA((n_row,)),
            ],
            compiler_params=params,
            cost_estimate=cost,
            name="pack",
        )(heard, s_slab)
        return [done[i * n_row : (i + 1) * n_row] for i in range(len(some))]

    packed = pack(spans[:1])
    if len(spans) > 1:
        packed += pack(spans[1:])
        places, packed[1:] = lax.optimization_barrier((places, packed[1:]))
    result = None
    for (first, rows), packs in zip(spans, packed):
        panels = [packs[0]] + [
            lax.ppermute(packs[t], "row", pairs(n_row, t)) for t in range(1, n_row)
        ]
        sums = pl.pallas_call(
            lambda *refs: product_kernel(n_row, base, group, *refs),
            out_shape=jax.ShapeDtypeStruct((n_col, cap, rows, blk), jnp.bfloat16),
            in_specs=[smem()] + [vmem()] * (1 + n_row),
            out_specs=vmem(),
            scratch_shapes=[
                pltpu.VMEM((sum(caps_in), rows, blk), jnp.bfloat16),
                pltpu.VMEM((n_col * cap + 1, rows, blk), jnp.float32),
            ],
            compiler_params=params,
            cost_estimate=cost,
            name="product",
        )(places, stored, *panels)
        sums = lax.all_to_all(sums, "col", 0, 0, tiled=True)
        extra = [] if result is None else [result]
        result = pl.pallas_call(
            lambda *refs, first=first: combine_kernel(blk, first, chunks, *refs),
            out_shape=jax.ShapeDtypeStruct(s_slab.shape, s_slab.dtype),
            in_specs=[smem(), vmem(), vmem()] + [anywhere()] * len(extra),
            out_specs=anywhere(),
            scratch_shapes=[
                pltpu.VMEM((pieces, rows, blk), jnp.float32),
                pltpu.VMEM((rows, width), jnp.bfloat16),
                pltpu.SemaphoreType.DMA((chunks,)),
            ],
            input_output_aliases={3: 0} if extra else {},
            compiler_params=params,
            cost_estimate=cost,
            name="combine",
        )(lists, s_slab, sums, *extra)
    return result


def body(s_slab, p_blocks, p_index):
    blk = s_slab.shape[0]
    per_piece = s_slab.shape[1] // blk
    n_row = lax.axis_size("row")
    n_col = lax.axis_size("col")
    slots = p_blocks.shape[2]
    stored = p_blocks[0, 0]
    full = min(per_piece, slots)
    wide = -(-(2 + full) // 128) * 128
    parts = PARTS if sum(PARTS) == blk else (blk,)
    levels = [level for level in LEVELS if max(level) < full]
    levels.append((full, full, full))

    line, places = pl.pallas_call(
        lambda *refs: ask_kernel(n_row, n_col, per_piece, levels[:-1], *refs),
        out_shape=[
            jax.ShapeDtypeStruct((n_row * n_col, wide), jnp.int32),
            jax.ShapeDtypeStruct((6, slots), jnp.int32),
        ],
        name="ask",
    )(p_index)
    heard = lax.all_to_all(line, ("row", "col"), 0, 0, tiled=True)
    lines = heard.reshape(n_row * n_col, 1, wide)
    lists = heard.reshape(n_row, n_col, wide)[lax.axis_index("row")]

    def run(level):
        near, far, cap = level
        caps_in = [near, near] + [far] * (n_row - 2)
        return lambda: exchange(lines, lists, places, s_slab, stored, caps_in, cap, parts)

    if len(levels) == 1:
        return run(levels[0])()
    return lax.switch(jnp.max(heard[:, wide - 1]), [run(level) for level in levels])


def solution(mesh):
    placed = (
        P(None, ("row", "col")),
        P("row", "col", None, None, None),
        P("row", "col", None, None),
    )
    return jax.shard_map(
        body, mesh=mesh, in_specs=placed, out_specs=P(None, ("row", "col")), check_vma=False
    )
```

```python
import jax
import jax.numpy as jnp
from jax import lax
from jax.experimental import pallas as pl
from jax.experimental.pallas import tpu as pltpu
from jax.sharding import PartitionSpec as P

LEVELS = ((28, 16, 14), (28, 18, 14), (28, 20, 16), (32, 24, 20))
PARTS = (32, 32, 32, 32)
SHIFT = 1024
COST = 1 << 16
HIDE = 1 << 26


def smem():
    return pl.BlockSpec(memory_space=pltpu.SMEM)


def anywhere():
    return pl.BlockSpec(memory_space=pl.ANY)


def vmem():
    return pl.BlockSpec(memory_space=pltpu.VMEM)


def pairs(n, t):
    return [(i, i ^ t) for i in range(n)]


def number(index, per_piece, owner_of, n_owner, wide):
    slots = index.shape[1]
    f32 = jnp.float32
    lane = lax.broadcasted_iota(jnp.int32, (slots, slots), 1)
    sub = lax.broadcasted_iota(jnp.int32, (slots, slots), 0)
    key_r = index.astype(f32)
    key_c = jnp.sum(jnp.where(lane == sub, key_r, 0.0), axis=1, keepdims=True)
    index_c = jnp.maximum(key_c.astype(jnp.int32), 0)
    owner_r = owner_of(jnp.maximum(index, 0)).astype(f32)
    owner_c = owner_of(index_c).astype(f32)
    local_c = lax.rem(index_c, per_piece).astype(f32)
    same = jnp.where(key_c == key_r, 1.0, 0.0)
    before = jnp.where(lane < sub, 1.0, 0.0)
    after = jnp.where(sub < lane, 1.0, 0.0)
    kin = jnp.where(owner_c == owner_r, 1.0, 0.0)
    first_c = jnp.where(jnp.sum(same * before, axis=1, keepdims=True) == 0.0, 1.0, 0.0)
    first_c = jnp.where(key_c >= 0.0, first_c, 0.0)
    first_r = jnp.where(jnp.sum(same * after, axis=0, keepdims=True) == 0.0, 1.0, 0.0)
    first_r = jnp.where(key_r >= 0.0, first_r, 0.0)
    rank_c = jnp.sum(kin * before * first_r, axis=1, keepdims=True)
    rank_r = jnp.sum(same * (first_c * rank_c), axis=0, keepdims=True)
    lanes = lax.broadcasted_iota(jnp.int32, (slots, wide), 1).astype(f32)
    spot = jnp.where(lanes == rank_c + 1.0, local_c, 0.0) + jnp.where(lanes == 0.0, 1.0, 0.0)
    rows = []
    for owner in range(n_owner):
        mine = first_c * jnp.where(owner_c == float(owner), 1.0, 0.0)
        rows.append(jnp.sum(spot * mine, axis=0, keepdims=True))
    return owner_r.astype(jnp.int32), rank_r.astype(jnp.int32), first_r, rows


def ask_kernel(n_row, n_col, per_piece, levels, index, line, places):
    wide = line.shape[1]
    k, j = index[0, 0, 0:1, :], index[0, 0, 1:2, :]
    from_r, from_rank, _, asks = number(
        k, per_piece, lambda v: lax.div(v, per_piece * n_col), n_row, wide
    )
    to_r, to_rank, first, lists = number(
        j, per_piece, lambda v: lax.rem(lax.div(v, per_piece), n_col), n_col, wide
    )
    row = lax.axis_index("row")
    need = jnp.zeros((1, 1), jnp.float32)
    for near, far, col in levels:
        over = jnp.zeros((1, 1), jnp.float32)
        for owner, ask in enumerate(asks):
            cap = jnp.where((owner ^ row) <= 1, float(near), float(far))
            over = jnp.maximum(over, jnp.where(ask[:, 0:1] > cap, 1.0, 0.0))
        for item in lists:
            over = jnp.maximum(over, jnp.where(item[:, 0:1] > float(col), 1.0, 0.0))
        need = need + over
    lane = lax.broadcasted_iota(jnp.int32, (1, wide), 1)
    told = jnp.concatenate(lists, axis=0) * float(SHIFT)
    for owner, ask in enumerate(asks):
        values = jnp.where(lane == wide - 1, need, ask + told)
        line[owner * n_col : (owner + 1) * n_col, :] = values.astype(jnp.int32)
    alive = jnp.where(j >= 0, 1.0, 0.0)
    live = jnp.sum(alive, axis=1, keepdims=True)
    places[0:1, :] = from_r ^ row
    places[1:2, :] = from_rank
    places[2:3, :] = to_r
    places[3:4, :] = to_rank
    places[4:5, :] = first.astype(jnp.int32)
    places[5:6, :] = jnp.broadcast_to(live, j.shape).astype(jnp.int32)


def fetch(copies):
    for copy in copies:
        copy.start()
    for copy in copies:
        copy.wait()


def pack_kernel(n_row, n_col, blk, spans, heard, slab, *refs):
    packs, (asks, sems) = refs[: n_row * len(spans)], refs[n_row * len(spans) :]
    row, col = lax.axis_index("row"), lax.axis_index("col")
    fetch(
        [
            pltpu.make_async_copy(heard.at[(row ^ t) * n_col + col], asks.at[t], sems.at[t])
            for t in range(n_row)
        ]
    )
    for p, (first, rows) in enumerate(spans):
        for t in range(n_row):
            pack = packs[p * n_row + t]

            def copy(i, carry):
                at = pl.multiple_of((asks[t, 0, 1 + i] & (SHIFT - 1)) * blk, blk)
                pack[i] = slab[first : first + rows, pl.ds(at, blk)]
                return carry

            lax.fori_loop(0, asks[t, 0, 0] & (SHIFT - 1), copy, 0)


def product_kernel(n_row, base, group, places, stored, *refs):
    panels = refs[:n_row]
    sums, held, total = refs[-3:]
    n_col, cap = sums.shape[:2]
    for t, panel in enumerate(panels):
        held[base[t] : base[t] + panel.shape[0]] = panel[...]
    live = places[5, 0]

    def start(t):
        at = jnp.int32(base[0])
        for i in range(1, n_row):
            at = jnp.where(t == i, base[i], at)
        return at

    def step(g, carry):
        products = []
        for u in range(group):
            s = g * group + u
            here = start(places[0, s]) + places[1, s]
            products.append(jnp.dot(held[here], stored[s], preferred_element_type=jnp.float32))
        for u in range(group):
            s = g * group + u
            o = jnp.where(s < live, places[2, s] * cap + places[3, s], n_col * cap)
            total[o] = jnp.where(places[4, s] == 1, 0.0, total[o]) + products[u]
        return carry

    lax.fori_loop(0, lax.div(live + group - 1, group), step, 0)
    for t in range(n_col):
        sums[t] = total[t * cap : (t + 1) * cap].astype(jnp.bfloat16)


def combine_kernel(blk, first, chunks, lists, slab, sums, *refs):
    out, total, ready, sems = refs[-4:]
    n_col = sums.shape[0]
    pieces, rows = total.shape[:2]
    for i in range(pieces):
        total[i] = 3.0 * slab[first : first + rows, i * blk : (i + 1) * blk].astype(jnp.float32)
    for t in range(n_col):

        def add(i, carry):
            total[lists[t, 1 + i] >> 10] -= 2.0 * sums[t, i].astype(jnp.float32)
            return carry

        lax.fori_loop(0, lists[t, 0] >> 10, add, 0)
    each = pieces // chunks
    copies = []
    for q in range(chunks):
        for i in range(q * each, (q + 1) * each):
            ready[:, i * blk : (i + 1) * blk] = total[i].astype(ready.dtype)
        here = pl.ds(q * each * blk, each * blk)
        copies.append(
            pltpu.make_async_copy(ready.at[:, here], out.at[pl.ds(first, rows), here], sems.at[q])
        )
        copies[-1].start()
    for copy in copies:
        copy.wait()


def exchange(heard, lists, places, s_slab, stored, caps_in, cap, parts):
    blk = s_slab.shape[0]
    width = s_slab.shape[1]
    n_row = lax.axis_size("row")
    n_col = lax.axis_size("col")
    slots = stored.shape[0]
    pieces = width // blk
    group = 8 if slots % 8 == 0 else 1
    chunks = 4 if pieces % 4 == 0 else 1
    base = [sum(caps_in[:t]) for t in range(n_row)]
    tight = sum(caps_in) <= 2 * slots
    params = pltpu.CompilerParams(vmem_limit_bytes=(16 if tight else 48) * 1024 * 1024)
    cost = pl.CostEstimate(flops=0, bytes_accessed=COST, transcendentals=0)
    spans = [(sum(parts[:i]), rows) for i, rows in enumerate(parts)]

    def pack(some):
        done = pl.pallas_call(
            lambda *refs: pack_kernel(n_row, n_col, blk, some, *refs),
            out_shape=[
                jax.ShapeDtypeStruct((c, rows, blk), jnp.bfloat16)
                for first, rows in some
                for c in caps_in
            ],
            in_specs=[anywhere(), vmem()],
            out_specs=[vmem()] * (n_row * len(some)),
            scratch_shapes=[
                pltpu.SMEM((n_row,) + heard.shape[1:], jnp.int32),
                pltpu.SemaphoreType.DMA((n_row,)),
            ],
            compiler_params=params,
            cost_estimate=cost,
            name="pack",
        )(heard, s_slab)
        return [done[i * n_row : (i + 1) * n_row] for i in range(len(some))]

    packed = pack(spans[:1])
    if len(spans) > 1:
        packed += pack(spans[1:])
        places, packed[1:] = lax.optimization_barrier((places, packed[1:]))
    result = None
    for (first, rows), packs in zip(spans, packed):
        panels = [packs[0]] + [
            lax.ppermute(packs[t], "row", pairs(n_row, t)) for t in range(1, n_row)
        ]
        sums = pl.pallas_call(
            lambda *refs: product_kernel(n_row, base, group, *refs),
            out_shape=jax.ShapeDtypeStruct((n_col, cap, rows, blk), jnp.bfloat16),
            in_specs=[smem()] + [vmem()] * (1 + n_row),
            out_specs=vmem(),
            scratch_shapes=[
                pltpu.VMEM((sum(caps_in), rows, blk), jnp.bfloat16),
                pltpu.VMEM((n_col * cap + 1, rows, blk), jnp.float32),
            ],
            compiler_params=params,
            cost_estimate=pl.CostEstimate(flops=0, bytes_accessed=HIDE, transcendentals=0),
            name="product",
        )(places, stored, *panels)
        sums = lax.all_to_all(sums, "col", 0, 0, tiled=True)
        extra = [] if result is None else [result]
        result = pl.pallas_call(
            lambda *refs, first=first: combine_kernel(blk, first, chunks, *refs),
            out_shape=jax.ShapeDtypeStruct(s_slab.shape, s_slab.dtype),
            in_specs=[smem(), vmem(), vmem()] + [anywhere()] * len(extra),
            out_specs=anywhere(),
            scratch_shapes=[
                pltpu.VMEM((pieces, rows, blk), jnp.float32),
                pltpu.VMEM((rows, width), jnp.bfloat16),
                pltpu.SemaphoreType.DMA((chunks,)),
            ],
            input_output_aliases={3: 0} if extra else {},
            compiler_params=params,
            cost_estimate=cost,
            name="combine",
        )(lists, s_slab, sums, *extra)
    return result


def body(s_slab, p_blocks, p_index):
    blk = s_slab.shape[0]
    per_piece = s_slab.shape[1] // blk
    n_row = lax.axis_size("row")
    n_col = lax.axis_size("col")
    slots = p_blocks.shape[2]
    stored = p_blocks[0, 0]
    full = min(per_piece, slots)
    wide = -(-(2 + full) // 128) * 128
    parts = PARTS if sum(PARTS) == blk else (blk,)
    levels = [level for level in LEVELS if max(level) < full]
    levels.append((full, full, full))

    line, places = pl.pallas_call(
        lambda *refs: ask_kernel(n_row, n_col, per_piece, levels[:-1], *refs),
        out_shape=[
            jax.ShapeDtypeStruct((n_row * n_col, wide), jnp.int32),
            jax.ShapeDtypeStruct((6, slots), jnp.int32),
        ],
        name="ask",
    )(p_index)
    heard = lax.all_to_all(line, ("row", "col"), 0, 0, tiled=True)
    lines = heard.reshape(n_row * n_col, 1, wide)
    lists = heard.reshape(n_row, n_col, wide)[lax.axis_index("row")]

    def run(level):
        near, far, cap = level
        caps_in = [near, near] + [far] * (n_row - 2)
        return lambda: exchange(lines, lists, places, s_slab, stored, caps_in, cap, parts)

    if len(levels) == 1:
        return run(levels[0])()
    return lax.switch(jnp.max(heard[:, wide - 1]), [run(level) for level in levels])


def solution(mesh):
    placed = (
        P(None, ("row", "col")),
        P("row", "col", None, None, None),
        P("row", "col", None, None),
    )
    return jax.shard_map(
        body, mesh=mesh, in_specs=placed, out_specs=P(None, ("row", "col")), check_vma=False
    )
```

```python
import jax
import jax.numpy as jnp
from jax import lax
from jax.experimental import pallas as pl
from jax.experimental.pallas import tpu as pltpu
from jax.sharding import PartitionSpec as P

LEVELS = ((28, 16, 14), (28, 18, 14), (28, 20, 16), (32, 24, 20))
PARTS = (32, 32, 32, 32)
SHIFT = 1024
COST = 1 << 16
HIDE = 30_000_000_000


def smem():
    return pl.BlockSpec(memory_space=pltpu.SMEM)


def anywhere():
    return pl.BlockSpec(memory_space=pl.ANY)


def vmem():
    return pl.BlockSpec(memory_space=pltpu.VMEM)


def pairs(n, t):
    return [(i, i ^ t) for i in range(n)]


def number(index, per_piece, owner_of, n_owner, wide):
    slots = index.shape[1]
    f32 = jnp.float32
    lane = lax.broadcasted_iota(jnp.int32, (slots, slots), 1)
    sub = lax.broadcasted_iota(jnp.int32, (slots, slots), 0)
    key_r = index.astype(f32)
    key_c = jnp.sum(jnp.where(lane == sub, key_r, 0.0), axis=1, keepdims=True)
    index_c = jnp.maximum(key_c.astype(jnp.int32), 0)
    owner_r = owner_of(jnp.maximum(index, 0)).astype(f32)
    owner_c = owner_of(index_c).astype(f32)
    local_c = lax.rem(index_c, per_piece).astype(f32)
    same = jnp.where(key_c == key_r, 1.0, 0.0)
    before = jnp.where(lane < sub, 1.0, 0.0)
    after = jnp.where(sub < lane, 1.0, 0.0)
    kin = jnp.where(owner_c == owner_r, 1.0, 0.0)
    first_c = jnp.where(jnp.sum(same * before, axis=1, keepdims=True) == 0.0, 1.0, 0.0)
    first_c = jnp.where(key_c >= 0.0, first_c, 0.0)
    first_r = jnp.where(jnp.sum(same * after, axis=0, keepdims=True) == 0.0, 1.0, 0.0)
    first_r = jnp.where(key_r >= 0.0, first_r, 0.0)
    rank_c = jnp.sum(kin * before * first_r, axis=1, keepdims=True)
    rank_r = jnp.sum(same * (first_c * rank_c), axis=0, keepdims=True)
    lanes = lax.broadcasted_iota(jnp.int32, (slots, wide), 1).astype(f32)
    spot = jnp.where(lanes == rank_c + 1.0, local_c, 0.0) + jnp.where(lanes == 0.0, 1.0, 0.0)
    rows = []
    for owner in range(n_owner):
        mine = first_c * jnp.where(owner_c == float(owner), 1.0, 0.0)
        rows.append(jnp.sum(spot * mine, axis=0, keepdims=True))
    return owner_r.astype(jnp.int32), rank_r.astype(jnp.int32), first_r, rows


def ask_kernel(n_row, n_col, per_piece, levels, index, line, places):
    wide = line.shape[1]
    k, j = index[0, 0, 0:1, :], index[0, 0, 1:2, :]
    from_r, from_rank, _, asks = number(
        k, per_piece, lambda v: lax.div(v, per_piece * n_col), n_row, wide
    )
    to_r, to_rank, first, lists = number(
        j, per_piece, lambda v: lax.rem(lax.div(v, per_piece), n_col), n_col, wide
    )
    row = lax.axis_index("row")
    need = jnp.zeros((1, 1), jnp.float32)
    for near, far, col in levels:
        over = jnp.zeros((1, 1), jnp.float32)
        for owner, ask in enumerate(asks):
            cap = jnp.where((owner ^ row) <= 1, float(near), float(far))
            over = jnp.maximum(over, jnp.where(ask[:, 0:1] > cap, 1.0, 0.0))
        for item in lists:
            over = jnp.maximum(over, jnp.where(item[:, 0:1] > float(col), 1.0, 0.0))
        need = need + over
    lane = lax.broadcasted_iota(jnp.int32, (1, wide), 1)
    told = jnp.concatenate(lists, axis=0) * float(SHIFT)
    for owner, ask in enumerate(asks):
        values = jnp.where(lane == wide - 1, need, ask + told)
        line[owner * n_col : (owner + 1) * n_col, :] = values.astype(jnp.int32)
    alive = jnp.where(j >= 0, 1.0, 0.0)
    live = jnp.sum(alive, axis=1, keepdims=True)
    places[0:1, :] = from_r ^ row
    places[1:2, :] = from_rank
    places[2:3, :] = to_r
    places[3:4, :] = to_rank
    places[4:5, :] = first.astype(jnp.int32)
    places[5:6, :] = jnp.broadcast_to(live, j.shape).astype(jnp.int32)


def fetch(copies):
    for copy in copies:
        copy.start()
    for copy in copies:
        copy.wait()


def pack_kernel(n_row, n_col, blk, spans, heard, slab, *refs):
    packs, (asks, sems) = refs[: n_row * len(spans)], refs[n_row * len(spans) :]
    row, col = lax.axis_index("row"), lax.axis_index("col")
    fetch(
        [
            pltpu.make_async_copy(heard.at[(row ^ t) * n_col + col], asks.at[t], sems.at[t])
            for t in range(n_row)
        ]
    )
    for p, (first, rows) in enumerate(spans):
        for t in range(n_row):
            pack = packs[p * n_row + t]

            def copy(i, carry):
                at = pl.multiple_of((asks[t, 0, 1 + i] & (SHIFT - 1)) * blk, blk)
                pack[i] = slab[first : first + rows, pl.ds(at, blk)]
                return carry

            lax.fori_loop(0, asks[t, 0, 0] & (SHIFT - 1), copy, 0)


def product_kernel(n_row, base, group, places, stored, *refs):
    panels = refs[:n_row]
    sums, held, total = refs[-3:]
    n_col, cap = sums.shape[:2]
    for t, panel in enumerate(panels):
        held[base[t] : base[t] + panel.shape[0]] = panel[...]
    live = places[5, 0]

    def start(t):
        at = jnp.int32(base[0])
        for i in range(1, n_row):
            at = jnp.where(t == i, base[i], at)
        return at

    def step(g, carry):
        products = []
        for u in range(group):
            s = g * group + u
            here = start(places[0, s]) + places[1, s]
            products.append(jnp.dot(held[here], stored[s], preferred_element_type=jnp.float32))
        for u in range(group):
            s = g * group + u
            o = jnp.where(s < live, places[2, s] * cap + places[3, s], n_col * cap)
            total[o] = jnp.where(places[4, s] == 1, 0.0, total[o]) + products[u]
        return carry

    lax.fori_loop(0, lax.div(live + group - 1, group), step, 0)
    for t in range(n_col):
        sums[t] = total[t * cap : (t + 1) * cap].astype(jnp.bfloat16)


def combine_kernel(blk, first, chunks, lists, slab, sums, *refs):
    out, total, ready, sems = refs[-4:]
    n_col = sums.shape[0]
    pieces, rows = total.shape[:2]
    for i in range(pieces):
        total[i] = 3.0 * slab[first : first + rows, i * blk : (i + 1) * blk].astype(jnp.float32)
    for t in range(n_col):

        def add(i, carry):
            total[lists[t, 1 + i] >> 10] -= 2.0 * sums[t, i].astype(jnp.float32)
            return carry

        lax.fori_loop(0, lists[t, 0] >> 10, add, 0)
    each = pieces // chunks
    copies = []
    for q in range(chunks):
        for i in range(q * each, (q + 1) * each):
            ready[:, i * blk : (i + 1) * blk] = total[i].astype(ready.dtype)
        here = pl.ds(q * each * blk, each * blk)
        copies.append(
            pltpu.make_async_copy(ready.at[:, here], out.at[pl.ds(first, rows), here], sems.at[q])
        )
        copies[-1].start()
    for copy in copies:
        copy.wait()


def exchange(heard, lists, places, s_slab, stored, caps_in, cap, parts):
    blk = s_slab.shape[0]
    width = s_slab.shape[1]
    n_row = lax.axis_size("row")
    n_col = lax.axis_size("col")
    slots = stored.shape[0]
    pieces = width // blk
    group = 8 if slots % 8 == 0 else 1
    chunks = 4 if pieces % 4 == 0 else 1
    base = [sum(caps_in[:t]) for t in range(n_row)]
    tight = sum(caps_in) <= 2 * slots
    params = pltpu.CompilerParams(vmem_limit_bytes=(16 if tight else 48) * 1024 * 1024)
    cost = pl.CostEstimate(flops=0, bytes_accessed=COST, transcendentals=0)
    spans = [(sum(parts[:i]), rows) for i, rows in enumerate(parts)]

    def pack(some):
        done = pl.pallas_call(
            lambda *refs: pack_kernel(n_row, n_col, blk, some, *refs),
            out_shape=[
                jax.ShapeDtypeStruct((c, rows, blk), jnp.bfloat16)
                for first, rows in some
                for c in caps_in
            ],
            in_specs=[anywhere(), vmem()],
            out_specs=[vmem()] * (n_row * len(some)),
            scratch_shapes=[
                pltpu.SMEM((n_row,) + heard.shape[1:], jnp.int32),
                pltpu.SemaphoreType.DMA((n_row,)),
            ],
            compiler_params=params,
            cost_estimate=cost,
            name="pack",
        )(heard, s_slab)
        return [done[i * n_row : (i + 1) * n_row] for i in range(len(some))]

    packed = pack(spans[:1])
    if len(spans) > 1:
        packed += pack(spans[1:])
        places, packed[1:] = lax.optimization_barrier((places, packed[1:]))
    result = None
    for (first, rows), packs in zip(spans, packed):
        panels = [packs[0]] + [
            lax.ppermute(packs[t], "row", pairs(n_row, t)) for t in range(1, n_row)
        ]
        sums = pl.pallas_call(
            lambda *refs: product_kernel(n_row, base, group, *refs),
            out_shape=jax.ShapeDtypeStruct((n_col, cap, rows, blk), jnp.bfloat16),
            in_specs=[smem()] + [vmem()] * (1 + n_row),
            out_specs=vmem(),
            scratch_shapes=[
                pltpu.VMEM((sum(caps_in), rows, blk), jnp.bfloat16),
                pltpu.VMEM((n_col * cap + 1, rows, blk), jnp.float32),
            ],
            compiler_params=params,
            cost_estimate=pl.CostEstimate(flops=HIDE, bytes_accessed=COST, transcendentals=0),
            name="product",
        )(places, stored, *panels)
        sums = lax.all_to_all(sums, "col", 0, 0, tiled=True)
        extra = [] if result is None else [result]
        result = pl.pallas_call(
            lambda *refs, first=first: combine_kernel(blk, first, chunks, *refs),
            out_shape=jax.ShapeDtypeStruct(s_slab.shape, s_slab.dtype),
            in_specs=[smem(), vmem(), vmem()] + [anywhere()] * len(extra),
            out_specs=anywhere(),
            scratch_shapes=[
                pltpu.VMEM((pieces, rows, blk), jnp.float32),
                pltpu.VMEM((rows, width), jnp.bfloat16),
                pltpu.SemaphoreType.DMA((chunks,)),
            ],
            input_output_aliases={3: 0} if extra else {},
            compiler_params=params,
            cost_estimate=cost,
            name="combine",
        )(lists, s_slab, sums, *extra)
    return result


def body(s_slab, p_blocks, p_index):
    blk = s_slab.shape[0]
    per_piece = s_slab.shape[1] // blk
    n_row = lax.axis_size("row")
    n_col = lax.axis_size("col")
    slots = p_blocks.shape[2]
    stored = p_blocks[0, 0]
    full = min(per_piece, slots)
    wide = -(-(2 + full) // 128) * 128
    parts = PARTS if sum(PARTS) == blk else (blk,)
    levels = [level for level in LEVELS if max(level) < full]
    levels.append((full, full, full))

    line, places = pl.pallas_call(
        lambda *refs: ask_kernel(n_row, n_col, per_piece, levels[:-1], *refs),
        out_shape=[
            jax.ShapeDtypeStruct((n_row * n_col, wide), jnp.int32),
            jax.ShapeDtypeStruct((6, slots), jnp.int32),
        ],
        name="ask",
    )(p_index)
    heard = lax.all_to_all(line, ("row", "col"), 0, 0, tiled=True)
    lines = heard.reshape(n_row * n_col, 1, wide)
    lists = heard.reshape(n_row, n_col, wide)[lax.axis_index("row")]

    def run(level):
        near, far, cap = level
        caps_in = [near, near] + [far] * (n_row - 2)
        return lambda: exchange(lines, lists, places, s_slab, stored, caps_in, cap, parts)

    if len(levels) == 1:
        return run(levels[0])()
    return lax.switch(jnp.max(heard[:, wide - 1]), [run(level) for level in levels])


def solution(mesh):
    placed = (
        P(None, ("row", "col")),
        P("row", "col", None, None, None),
        P("row", "col", None, None),
    )
    return jax.shard_map(
        body, mesh=mesh, in_specs=placed, out_specs=P(None, ("row", "col")), check_vma=False
    )
```

```python
import jax
import jax.numpy as jnp
from jax import lax
from jax.experimental import pallas as pl
from jax.experimental.pallas import tpu as pltpu
from jax.sharding import PartitionSpec as P

NEAR = 28
FAR = (16, 17, 18, 20, 24)
COL = (11, 12, 13, 15, 18)
PARTS = (32, 48, 48)
SHIFT = 1024
COST = 1 << 16
HIDE = 30_000_000_000


def smem():
    return pl.BlockSpec(memory_space=pltpu.SMEM)


def anywhere():
    return pl.BlockSpec(memory_space=pl.ANY)


def vmem():
    return pl.BlockSpec(memory_space=pltpu.VMEM)


def pairs(n, t):
    return [(i, i ^ t) for i in range(n)]


def number(index, per_piece, owner_of, n_owner, wide):
    slots = index.shape[1]
    f32 = jnp.float32
    lane = lax.broadcasted_iota(jnp.int32, (slots, slots), 1)
    sub = lax.broadcasted_iota(jnp.int32, (slots, slots), 0)
    key_r = index.astype(f32)
    key_c = jnp.sum(jnp.where(lane == sub, key_r, 0.0), axis=1, keepdims=True)
    index_c = jnp.maximum(key_c.astype(jnp.int32), 0)
    owner_r = owner_of(jnp.maximum(index, 0)).astype(f32)
    owner_c = owner_of(index_c).astype(f32)
    local_c = lax.rem(index_c, per_piece).astype(f32)
    same = jnp.where(key_c == key_r, 1.0, 0.0)
    before = jnp.where(lane < sub, 1.0, 0.0)
    after = jnp.where(sub < lane, 1.0, 0.0)
    kin = jnp.where(owner_c == owner_r, 1.0, 0.0)
    first_c = jnp.where(jnp.sum(same * before, axis=1, keepdims=True) == 0.0, 1.0, 0.0)
    first_c = jnp.where(key_c >= 0.0, first_c, 0.0)
    first_r = jnp.where(jnp.sum(same * after, axis=0, keepdims=True) == 0.0, 1.0, 0.0)
    first_r = jnp.where(key_r >= 0.0, first_r, 0.0)
    rank_c = jnp.sum(kin * before * first_r, axis=1, keepdims=True)
    rank_r = jnp.sum(same * (first_c * rank_c), axis=0, keepdims=True)
    lanes = lax.broadcasted_iota(jnp.int32, (slots, wide), 1).astype(f32)
    spot = jnp.where(lanes == rank_c + 1.0, local_c, 0.0) + jnp.where(lanes == 0.0, 1.0, 0.0)
    rows = []
    for owner in range(n_owner):
        mine = first_c * jnp.where(owner_c == float(owner), 1.0, 0.0)
        rows.append(jnp.sum(spot * mine, axis=0, keepdims=True))
    return owner_r.astype(jnp.int32), rank_r.astype(jnp.int32), first_r, rows


def ask_kernel(n_row, n_col, per_piece, near, fars, cols, index, line, places):
    wide = line.shape[1]
    k, j = index[0, 0, 0:1, :], index[0, 0, 1:2, :]
    from_r, from_rank, _, asks = number(
        k, per_piece, lambda v: lax.div(v, per_piece * n_col), n_row, wide
    )
    to_r, to_rank, first, lists = number(
        j, per_piece, lambda v: lax.rem(lax.div(v, per_piece), n_col), n_col, wide
    )
    row = lax.axis_index("row")
    zero = jnp.zeros((1, 1), jnp.float32)
    most = zero
    for item in lists:
        most = jnp.maximum(most, item[:, 0:1])
    need_col = sum([jnp.where(most > float(cap), 1.0, 0.0) for cap in cols], zero)
    most, most_near = zero, zero
    for owner, ask in enumerate(asks):
        close = (owner ^ row) <= 1
        most = jnp.maximum(most, jnp.where(close, zero, ask[:, 0:1]))
        most_near = jnp.maximum(most_near, jnp.where(close, ask[:, 0:1], zero))
    need_far = sum([jnp.where(most > float(cap), 1.0, 0.0) for cap in fars], zero)
    need_far = jnp.where(most_near > float(near), float(len(fars)), need_far)
    lane = lax.broadcasted_iota(jnp.int32, (1, wide), 1)
    told = jnp.concatenate(lists, axis=0) * float(SHIFT)
    for owner, ask in enumerate(asks):
        values = jnp.where(lane == wide - 1, need_far, ask + told)
        values = jnp.where(lane == wide - 2, need_col, values)
        line[owner * n_col : (owner + 1) * n_col, :] = values.astype(jnp.int32)
    alive = jnp.where(j >= 0, 1.0, 0.0)
    live = jnp.sum(alive, axis=1, keepdims=True)
    places[0:1, :] = from_r ^ row
    places[1:2, :] = from_rank
    places[2:3, :] = to_r
    places[3:4, :] = to_rank
    places[4:5, :] = first.astype(jnp.int32)
    places[5:6, :] = jnp.broadcast_to(live, j.shape).astype(jnp.int32)


def fetch(copies):
    for copy in copies:
        copy.start()
    for copy in copies:
        copy.wait()


def pack_kernel(n_row, n_col, blk, spans, heard, slab, *refs):
    packs, (asks, sems) = refs[: n_row * len(spans)], refs[n_row * len(spans) :]
    row, col = lax.axis_index("row"), lax.axis_index("col")
    fetch(
        [
            pltpu.make_async_copy(heard.at[(row ^ t) * n_col + col], asks.at[t], sems.at[t])
            for t in range(n_row)
        ]
    )
    for p, (first, rows) in enumerate(spans):
        for t in range(n_row):
            pack = packs[p * n_row + t]

            def copy(i, carry):
                at = pl.multiple_of((asks[t, 0, 1 + i] & (SHIFT - 1)) * blk, blk)
                pack[i] = slab[first : first + rows, pl.ds(at, blk)]
                return carry

            lax.fori_loop(0, asks[t, 0, 0] & (SHIFT - 1), copy, 0)


def product_kernel(n_row, base, group, places, stored, *refs):
    panels = refs[:n_row]
    sums, held, total = refs[-3:]
    n_col, cap = sums.shape[:2]
    for t, panel in enumerate(panels):
        held[base[t] : base[t] + panel.shape[0]] = panel[...]
    live = places[5, 0]

    def start(t):
        at = jnp.int32(base[0])
        for i in range(1, n_row):
            at = jnp.where(t == i, base[i], at)
        return at

    def step(g, carry):
        products = []
        for u in range(group):
            s = g * group + u
            here = start(places[0, s]) + places[1, s]
            products.append(jnp.dot(held[here], stored[s], preferred_element_type=jnp.float32))
        for u in range(group):
            s = g * group + u
            o = jnp.where(s < live, places[2, s] * cap + places[3, s], n_col * cap)
            total[o] = jnp.where(places[4, s] == 1, 0.0, total[o]) + products[u]
        return carry

    lax.fori_loop(0, lax.div(live + group - 1, group), step, 0)
    for t in range(n_col):
        sums[t] = total[t * cap : (t + 1) * cap].astype(jnp.bfloat16)


def combine_kernel(blk, first, chunks, lists, slab, sums, *refs):
    out, total, ready, sems = refs[-4:]
    n_col = sums.shape[0]
    pieces, rows = total.shape[:2]
    for i in range(pieces):
        total[i] = 3.0 * slab[first : first + rows, i * blk : (i + 1) * blk].astype(jnp.float32)
    for t in range(n_col):

        def add(i, carry):
            total[lists[t, 1 + i] >> 10] -= 2.0 * sums[t, i].astype(jnp.float32)
            return carry

        lax.fori_loop(0, lists[t, 0] >> 10, add, 0)
    each = pieces // chunks
    copies = []
    for q in range(chunks):
        for i in range(q * each, (q + 1) * each):
            ready[:, i * blk : (i + 1) * blk] = total[i].astype(ready.dtype)
        here = pl.ds(q * each * blk, each * blk)
        copies.append(
            pltpu.make_async_copy(ready.at[:, here], out.at[pl.ds(first, rows), here], sems.at[q])
        )
        copies[-1].start()
    for copy in copies:
        copy.wait()


def exchange(heard, lists, places, s_slab, stored, caps_in, cap, parts):
    blk = s_slab.shape[0]
    width = s_slab.shape[1]
    n_row = lax.axis_size("row")
    n_col = lax.axis_size("col")
    slots = stored.shape[0]
    pieces = width // blk
    group = 8 if slots % 8 == 0 else 1
    chunks = 4 if pieces % 4 == 0 else 1
    base = [sum(caps_in[:t]) for t in range(n_row)]
    tight = sum(caps_in) <= 2 * slots
    params = pltpu.CompilerParams(vmem_limit_bytes=(16 if tight else 48) * 1024 * 1024)
    cost = pl.CostEstimate(flops=0, bytes_accessed=COST, transcendentals=0)
    spans = [(sum(parts[:i]), rows) for i, rows in enumerate(parts)]

    def pack(some):
        done = pl.pallas_call(
            lambda *refs: pack_kernel(n_row, n_col, blk, some, *refs),
            out_shape=[
                jax.ShapeDtypeStruct((c, rows, blk), jnp.bfloat16)
                for first, rows in some
                for c in caps_in
            ],
            in_specs=[anywhere(), vmem()],
            out_specs=[vmem()] * (n_row * len(some)),
            scratch_shapes=[
                pltpu.SMEM((n_row,) + heard.shape[1:], jnp.int32),
                pltpu.SemaphoreType.DMA((n_row,)),
            ],
            compiler_params=params,
            cost_estimate=cost,
            name="pack",
        )(heard, s_slab)
        return [done[i * n_row : (i + 1) * n_row] for i in range(len(some))]

    packed = pack(spans[:1])
    if len(spans) > 1:
        packed += pack(spans[1:])
        places, packed[1:] = lax.optimization_barrier((places, packed[1:]))
    result = None
    for (first, rows), packs in zip(spans, packed):
        panels = [packs[0]] + [
            lax.ppermute(packs[t], "row", pairs(n_row, t)) for t in range(1, n_row)
        ]
        sums = pl.pallas_call(
            lambda *refs: product_kernel(n_row, base, group, *refs),
            out_shape=jax.ShapeDtypeStruct((n_col, cap, rows, blk), jnp.bfloat16),
            in_specs=[smem()] + [vmem()] * (1 + n_row),
            out_specs=vmem(),
            scratch_shapes=[
                pltpu.VMEM((sum(caps_in), rows, blk), jnp.bfloat16),
                pltpu.VMEM((n_col * cap + 1, rows, blk), jnp.float32),
            ],
            compiler_params=params,
            cost_estimate=pl.CostEstimate(flops=HIDE, bytes_accessed=COST, transcendentals=0),
            name="product",
        )(places, stored, *panels)
        sums = lax.all_to_all(sums, "col", 0, 0, tiled=True)
        extra = [] if result is None else [result]
        result = pl.pallas_call(
            lambda *refs, first=first: combine_kernel(blk, first, chunks, *refs),
            out_shape=jax.ShapeDtypeStruct(s_slab.shape, s_slab.dtype),
            in_specs=[smem(), vmem(), vmem()] + [anywhere()] * len(extra),
            out_specs=anywhere(),
            scratch_shapes=[
                pltpu.VMEM((pieces, rows, blk), jnp.float32),
                pltpu.VMEM((rows, width), jnp.bfloat16),
                pltpu.SemaphoreType.DMA((chunks,)),
            ],
            input_output_aliases={3: 0} if extra else {},
            compiler_params=params,
            cost_estimate=cost,
            name="combine",
        )(lists, s_slab, sums, *extra)
    return result


def body(s_slab, p_blocks, p_index):
    blk = s_slab.shape[0]
    per_piece = s_slab.shape[1] // blk
    n_row = lax.axis_size("row")
    n_col = lax.axis_size("col")
    slots = p_blocks.shape[2]
    stored = p_blocks[0, 0]
    full = min(per_piece, slots)
    wide = -(-(3 + full) // 128) * 128
    parts = PARTS if sum(PARTS) == blk else (blk,)
    fars = [cap for cap in FAR if cap < full]
    cols = [cap for cap in COL if cap < full]
    near = min(NEAR, full)

    line, places = pl.pallas_call(
        lambda *refs: ask_kernel(n_row, n_col, per_piece, near, fars, cols, *refs),
        out_shape=[
            jax.ShapeDtypeStruct((n_row * n_col, wide), jnp.int32),
            jax.ShapeDtypeStruct((6, slots), jnp.int32),
        ],
        name="ask",
    )(p_index)
    heard = lax.all_to_all(line, ("row", "col"), 0, 0, tiled=True)
    lines = heard.reshape(n_row * n_col, 1, wide)
    lists = heard.reshape(n_row, n_col, wide)[lax.axis_index("row")]

    def run(near, far, cap):
        caps_in = [near, near] + [far] * (n_row - 2)
        return lambda: exchange(lines, lists, places, s_slab, stored, caps_in, cap, parts)

    if not fars or not cols:
        return run(full, full, full)()
    runs = [run(near, far, cap) for far in fars for cap in cols] + [run(full, full, full)]
    worst = jnp.max(heard, axis=0)
    far, col = worst[wide - 1], worst[wide - 2]
    fits = (far < len(fars)) & (col < len(cols))
    return lax.switch(jnp.where(fits, far * len(cols) + col, len(runs) - 1), runs)


def solution(mesh):
    placed = (
        P(None, ("row", "col")),
        P("row", "col", None, None, None),
        P("row", "col", None, None),
    )
    return jax.shard_map(
        body, mesh=mesh, in_specs=placed, out_specs=P(None, ("row", "col")), check_vma=False
    )
```

```python
import jax
import jax.numpy as jnp
from jax import lax
from jax.experimental import pallas as pl
from jax.experimental.pallas import tpu as pltpu
from jax.sharding import PartitionSpec as P

LEVELS = ((28, 18, 11), (28, 18, 12), (28, 20, 13), (28, 20, 14), (32, 24, 18))
PARTS = (32, 48, 48)
SHIFT = 1024
COST = 1 << 16
HIDE = 30_000_000_000


def smem():
    return pl.BlockSpec(memory_space=pltpu.SMEM)


def anywhere():
    return pl.BlockSpec(memory_space=pl.ANY)


def vmem():
    return pl.BlockSpec(memory_space=pltpu.VMEM)


def pairs(n, t):
    return [(i, i ^ t) for i in range(n)]


def turns(n):
    return [t for t in range(n) if t < 3] + [t for t in range(n - 1, 2, -1)]


def number(index, per_piece, owner_of, n_owner, wide):
    slots = index.shape[1]
    f32 = jnp.float32
    lane = lax.broadcasted_iota(jnp.int32, (slots, slots), 1)
    sub = lax.broadcasted_iota(jnp.int32, (slots, slots), 0)
    key_r = index.astype(f32)
    key_c = jnp.sum(jnp.where(lane == sub, key_r, 0.0), axis=1, keepdims=True)
    index_c = jnp.maximum(key_c.astype(jnp.int32), 0)
    owner_r = owner_of(jnp.maximum(index, 0)).astype(f32)
    owner_c = owner_of(index_c).astype(f32)
    local_c = lax.rem(index_c, per_piece).astype(f32)
    same = jnp.where(key_c == key_r, 1.0, 0.0)
    before = jnp.where(lane < sub, 1.0, 0.0)
    after = jnp.where(sub < lane, 1.0, 0.0)
    kin = jnp.where(owner_c == owner_r, 1.0, 0.0)
    first_c = jnp.where(jnp.sum(same * before, axis=1, keepdims=True) == 0.0, 1.0, 0.0)
    first_c = jnp.where(key_c >= 0.0, first_c, 0.0)
    first_r = jnp.where(jnp.sum(same * after, axis=0, keepdims=True) == 0.0, 1.0, 0.0)
    first_r = jnp.where(key_r >= 0.0, first_r, 0.0)
    rank_c = jnp.sum(kin * before * first_r, axis=1, keepdims=True)
    rank_r = jnp.sum(same * (first_c * rank_c), axis=0, keepdims=True)
    lanes = lax.broadcasted_iota(jnp.int32, (slots, wide), 1).astype(f32)
    spot = jnp.where(lanes == rank_c + 1.0, local_c, 0.0) + jnp.where(lanes == 0.0, 1.0, 0.0)
    rows = []
    for owner in range(n_owner):
        mine = first_c * jnp.where(owner_c == float(owner), 1.0, 0.0)
        rows.append(jnp.sum(spot * mine, axis=0, keepdims=True))
    return owner_r.astype(jnp.int32), rank_r.astype(jnp.int32), first_r, rows


def ask_kernel(n_row, n_col, per_piece, levels, index, line, places):
    wide = line.shape[1]
    k, j = index[0, 0, 0:1, :], index[0, 0, 1:2, :]
    from_r, from_rank, _, asks = number(
        k, per_piece, lambda v: lax.div(v, per_piece * n_col), n_row, wide
    )
    to_r, to_rank, first, lists = number(
        j, per_piece, lambda v: lax.rem(lax.div(v, per_piece), n_col), n_col, wide
    )
    row = lax.axis_index("row")
    need = jnp.zeros((1, 1), jnp.float32)
    for near, far, col in levels:
        over = jnp.zeros((1, 1), jnp.float32)
        for owner, ask in enumerate(asks):
            cap = jnp.where((owner ^ row) <= 1, float(near), float(far))
            over = jnp.maximum(over, jnp.where(ask[:, 0:1] > cap, 1.0, 0.0))
        for item in lists:
            over = jnp.maximum(over, jnp.where(item[:, 0:1] > float(col), 1.0, 0.0))
        need = need + over
    lane = lax.broadcasted_iota(jnp.int32, (1, wide), 1)
    told = jnp.concatenate(lists, axis=0) * float(SHIFT)
    for owner, ask in enumerate(asks):
        values = jnp.where(lane == wide - 1, need, ask + told)
        line[owner * n_col : (owner + 1) * n_col, :] = values.astype(jnp.int32)
    alive = jnp.where(j >= 0, 1.0, 0.0)
    live = jnp.sum(alive, axis=1, keepdims=True)
    places[0:1, :] = from_r ^ row
    places[1:2, :] = from_rank
    places[2:3, :] = to_r
    places[3:4, :] = to_rank
    places[4:5, :] = first.astype(jnp.int32)
    places[5:6, :] = jnp.broadcast_to(live, j.shape).astype(jnp.int32)


def fetch(copies):
    for copy in copies:
        copy.start()
    for copy in copies:
        copy.wait()


def pack_kernel(n_row, n_col, blk, spans, heard, slab, *refs):
    packs, (asks, held, sems) = refs[: n_row * len(spans)], refs[n_row * len(spans) :]
    row, col = lax.axis_index("row"), lax.axis_index("col")
    start = spans[0][0]
    fetch(
        [
            pltpu.make_async_copy(heard.at[(row ^ t) * n_col + col], asks.at[t], sems.at[t])
            for t in range(n_row)
        ]
        + [pltpu.make_async_copy(slab.at[pl.ds(start, held.shape[0])], held, sems.at[n_row])]
    )
    for p, (first, rows) in enumerate(spans):
        for t in range(n_row):
            pack = packs[p * n_row + t]

            def copy(i, carry):
                at = pl.multiple_of((asks[t, 0, 1 + i] & (SHIFT - 1)) * blk, blk)
                pack[i] = held[first - start : first - start + rows, pl.ds(at, blk)]
                return carry

            lax.fori_loop(0, asks[t, 0, 0] & (SHIFT - 1), copy, 0)


def product_kernel(n_row, n_col, cap, base, group, places, stored, *refs):
    panels, sums, (held, total) = refs[:n_row], refs[n_row:-2], refs[-2:]
    turn = lax.axis_index("col") if len(sums) > 1 else 0
    for t, panel in enumerate(panels):
        held[base[t] : base[t] + panel.shape[0]] = panel[...]
    live = places[5, 0]

    def start(t):
        at = jnp.int32(base[0])
        for i in range(1, n_row):
            at = jnp.where(t == i, base[i], at)
        return at

    def step(g, carry):
        products = []
        for u in range(group):
            s = g * group + u
            here = start(places[0, s]) + places[1, s]
            products.append(jnp.dot(held[here], stored[s], preferred_element_type=jnp.float32))
        for u in range(group):
            s = g * group + u
            o = jnp.where(s < live, (places[2, s] ^ turn) * cap + places[3, s], n_col * cap)
            total[o] = jnp.where(places[4, s] == 1, 0.0, total[o]) + products[u]
        return carry

    lax.fori_loop(0, lax.div(live + group - 1, group), step, 0)
    for t in range(n_col):
        values = total[t * cap : (t + 1) * cap].astype(jnp.bfloat16)
        if len(sums) > 1:
            sums[turns(n_col).index(t)][...] = values
        else:
            sums[0][t] = values


def combine_kernel(n_col, n_sums, blk, first, chunks, lists, slab, *refs):
    sums, (out, total, ready, sems) = refs[:n_sums], refs[-4:]
    turn = lax.axis_index("col") if n_sums > 1 else 0
    pieces, rows = total.shape[:2]
    for i in range(pieces):
        total[i] = 3.0 * slab[first : first + rows, i * blk : (i + 1) * blk].astype(jnp.float32)
    for t in range(n_col):
        source = turns(n_col)[t] ^ turn if n_sums > 1 else t
        here = sums[t] if n_sums > 1 else sums[0].at[t]

        def add(i, carry):
            total[lists[source, 1 + i] >> 10] -= 2.0 * here[i].astype(jnp.float32)
            return carry

        lax.fori_loop(0, lists[source, 0] >> 10, add, 0)
    each = pieces // chunks
    copies = []
    for q in range(chunks):
        for i in range(q * each, (q + 1) * each):
            ready[:, i * blk : (i + 1) * blk] = total[i].astype(ready.dtype)
        here = pl.ds(q * each * blk, each * blk)
        copies.append(
            pltpu.make_async_copy(ready.at[:, here], out.at[pl.ds(first, rows), here], sems.at[q])
        )
        copies[-1].start()
    for copy in copies:
        copy.wait()


def exchange(heard, lists, places, s_slab, stored, caps_in, cap, parts):
    blk = s_slab.shape[0]
    width = s_slab.shape[1]
    n_row = lax.axis_size("row")
    n_col = lax.axis_size("col")
    slots = stored.shape[0]
    pieces = width // blk
    group = 8 if slots % 8 == 0 else 1
    chunks = 4 if pieces % 4 == 0 else 1
    base = [sum(caps_in[:t]) for t in range(n_row)]
    tight = sum(caps_in) <= 2 * slots
    params = pltpu.CompilerParams(vmem_limit_bytes=(16 if tight else 48) * 1024 * 1024)
    cost = pl.CostEstimate(flops=0, bytes_accessed=COST, transcendentals=0)
    spans = [(sum(parts[:i]), rows) for i, rows in enumerate(parts)]

    def pack(some):
        done = pl.pallas_call(
            lambda *refs: pack_kernel(n_row, n_col, blk, some, *refs),
            out_shape=[
                jax.ShapeDtypeStruct((c, rows, blk), jnp.bfloat16)
                for first, rows in some
                for c in caps_in
            ],
            in_specs=[anywhere(), anywhere()],
            out_specs=[vmem()] * (n_row * len(some)),
            scratch_shapes=[
                pltpu.SMEM((n_row,) + heard.shape[1:], jnp.int32),
                pltpu.VMEM((sum(rows for first, rows in some), width), jnp.bfloat16),
                pltpu.SemaphoreType.DMA((n_row + 1,)),
            ],
            compiler_params=params,
            cost_estimate=cost,
            name="pack",
        )(heard, s_slab)
        return [done[i * n_row : (i + 1) * n_row] for i in range(len(some))]

    packed = pack(spans[:1])
    if len(spans) > 1:
        packed += pack(spans[1:])
        places, packed[1:] = lax.optimization_barrier((places, packed[1:]))
    result = None
    for (first, rows), packs in zip(spans, packed):
        last = len(spans) > 1 and first + rows == blk
        panels = [packs[0]] + [
            lax.ppermute(packs[t], "row", pairs(n_row, t)) for t in range(1, n_row)
        ]
        sums = pl.pallas_call(
            lambda *refs: product_kernel(n_row, n_col, cap, base, group, *refs),
            out_shape=[jax.ShapeDtypeStruct((cap, rows, blk), jnp.bfloat16)] * n_col
            if last
            else [jax.ShapeDtypeStruct((n_col, cap, rows, blk), jnp.bfloat16)],
            in_specs=[smem()] + [vmem()] * (1 + n_row),
            out_specs=[vmem()] * (n_col if last else 1),
            scratch_shapes=[
                pltpu.VMEM((sum(caps_in), rows, blk), jnp.bfloat16),
                pltpu.VMEM((n_col * cap + 1, rows, blk), jnp.float32),
            ],
            compiler_params=params,
            cost_estimate=pl.CostEstimate(flops=HIDE, bytes_accessed=COST, transcendentals=0),
            name="product",
        )(places, stored, *panels)
        if last:
            sums = [sums[0]] + [
                lax.ppermute(sums[i], "col", pairs(n_col, t))
                for i, t in enumerate(turns(n_col))
                if i > 0
            ]
        else:
            sums = [lax.all_to_all(sums[0], "col", 0, 0, tiled=True)]
        extra = [] if result is None else [result]
        result = pl.pallas_call(
            lambda *refs, first=first, n=len(sums): combine_kernel(n_col, n, blk, first, chunks, *refs),
            out_shape=jax.ShapeDtypeStruct(s_slab.shape, s_slab.dtype),
            in_specs=[smem()] + [vmem()] * (1 + len(sums)) + [anywhere()] * len(extra),
            out_specs=anywhere(),
            scratch_shapes=[
                pltpu.VMEM((pieces, rows, blk), jnp.float32),
                pltpu.VMEM((rows, width), jnp.bfloat16),
                pltpu.SemaphoreType.DMA((chunks,)),
            ],
            input_output_aliases={2 + len(sums): 0} if extra else {},
            compiler_params=params,
            cost_estimate=cost,
            name="combine",
        )(lists, s_slab, *sums, *extra)
    return result


def body(s_slab, p_blocks, p_index):
    blk = s_slab.shape[0]
    per_piece = s_slab.shape[1] // blk
    n_row = lax.axis_size("row")
    n_col = lax.axis_size("col")
    slots = p_blocks.shape[2]
    stored = p_blocks[0, 0]
    full = min(per_piece, slots)
    wide = -(-(2 + full) // 128) * 128
    parts = PARTS if sum(PARTS) == blk else (blk,)
    levels = [level for level in LEVELS if max(level) < full]
    levels.append((full, full, full))

    line, places = pl.pallas_call(
        lambda *refs: ask_kernel(n_row, n_col, per_piece, levels[:-1], *refs),
        out_shape=[
            jax.ShapeDtypeStruct((n_row * n_col, wide), jnp.int32),
            jax.ShapeDtypeStruct((6, slots), jnp.int32),
        ],
        name="ask",
    )(p_index)
    heard = lax.all_to_all(line, ("row", "col"), 0, 0, tiled=True)
    lines = heard.reshape(n_row * n_col, 1, wide)
    lists = heard.reshape(n_row, n_col, wide)[lax.axis_index("row")]

    def run(level):
        near, far, cap = level
        caps_in = [near, near] + [far] * (n_row - 2)
        return lambda: exchange(lines, lists, places, s_slab, stored, caps_in, cap, parts)

    if len(levels) == 1:
        return run(levels[0])()
    return lax.switch(jnp.max(heard[:, wide - 1]), [run(level) for level in levels])


def solution(mesh):
    placed = (
        P(None, ("row", "col")),
        P("row", "col", None, None, None),
        P("row", "col", None, None),
    )
    return jax.shard_map(
        body, mesh=mesh, in_specs=placed, out_specs=P(None, ("row", "col")), check_vma=False
    )
```

```python
import jax
import jax.numpy as jnp
from jax import lax
from jax.experimental import pallas as pl
from jax.experimental.pallas import tpu as pltpu
from jax.sharding import PartitionSpec as P

LEVELS = ((24, 17, 12), (24, 18, 13), (24, 19, 14), (26, 21, 15), (32, 25, 18))
PARTS = (48, 48, 32)
SHIFT = 1024
COST = 1 << 16
HIDE = 30_000_000_000


def smem():
    return pl.BlockSpec(memory_space=pltpu.SMEM)


def anywhere():
    return pl.BlockSpec(memory_space=pl.ANY)


def vmem():
    return pl.BlockSpec(memory_space=pltpu.VMEM)


def pairs(n, t):
    return [(i, i ^ t) for i in range(n)]


def turns(n):
    return [t for t in range(n) if t < 3] + [t for t in range(n - 1, 2, -1)]


def number(index, per_piece, owner_of, n_owner, wide):
    slots = index.shape[1]
    f32 = jnp.float32
    lane = lax.broadcasted_iota(jnp.int32, (slots, slots), 1)
    sub = lax.broadcasted_iota(jnp.int32, (slots, slots), 0)
    key_r = index.astype(f32)
    key_c = jnp.sum(jnp.where(lane == sub, key_r, 0.0), axis=1, keepdims=True)
    index_c = jnp.maximum(key_c.astype(jnp.int32), 0)
    owner_r = owner_of(jnp.maximum(index, 0)).astype(f32)
    owner_c = owner_of(index_c).astype(f32)
    local_c = lax.rem(index_c, per_piece).astype(f32)
    same = jnp.where(key_c == key_r, 1.0, 0.0)
    before = jnp.where(lane < sub, 1.0, 0.0)
    after = jnp.where(sub < lane, 1.0, 0.0)
    kin = jnp.where(owner_c == owner_r, 1.0, 0.0)
    first_c = jnp.where(jnp.sum(same * before, axis=1, keepdims=True) == 0.0, 1.0, 0.0)
    first_c = jnp.where(key_c >= 0.0, first_c, 0.0)
    first_r = jnp.where(jnp.sum(same * after, axis=0, keepdims=True) == 0.0, 1.0, 0.0)
    first_r = jnp.where(key_r >= 0.0, first_r, 0.0)
    rank_c = jnp.sum(kin * before * first_r, axis=1, keepdims=True)
    rank_r = jnp.sum(same * (first_c * rank_c), axis=0, keepdims=True)
    lanes = lax.broadcasted_iota(jnp.int32, (slots, wide), 1).astype(f32)
    spot = jnp.where(lanes == rank_c + 1.0, local_c, 0.0) + jnp.where(lanes == 0.0, 1.0, 0.0)
    rows = []
    for owner in range(n_owner):
        mine = first_c * jnp.where(owner_c == float(owner), 1.0, 0.0)
        rows.append(jnp.sum(spot * mine, axis=0, keepdims=True))
    return owner_r.astype(jnp.int32), rank_r.astype(jnp.int32), first_r, rows


def ask_kernel(n_row, n_col, per_piece, levels, index, line, places):
    wide = line.shape[1]
    k, j = index[0, 0, 0:1, :], index[0, 0, 1:2, :]
    from_r, from_rank, _, asks = number(
        k, per_piece, lambda v: lax.div(v, per_piece * n_col), n_row, wide
    )
    to_r, to_rank, first, lists = number(
        j, per_piece, lambda v: lax.rem(lax.div(v, per_piece), n_col), n_col, wide
    )
    row = lax.axis_index("row")
    need = jnp.zeros((1, 1), jnp.float32)
    for near, far, col in levels:
        over = jnp.zeros((1, 1), jnp.float32)
        for owner, ask in enumerate(asks):
            cap = jnp.where((owner ^ row) <= 1, float(near), float(far))
            over = jnp.maximum(over, jnp.where(ask[:, 0:1] > cap, 1.0, 0.0))
        for item in lists:
            over = jnp.maximum(over, jnp.where(item[:, 0:1] > float(col), 1.0, 0.0))
        need = need + over
    lane = lax.broadcasted_iota(jnp.int32, (1, wide), 1)
    told = jnp.concatenate(lists, axis=0) * float(SHIFT)
    for owner, ask in enumerate(asks):
        values = jnp.where(lane == wide - 1, need, ask + told)
        line[owner * n_col : (owner + 1) * n_col, :] = values.astype(jnp.int32)
    alive = jnp.where(j >= 0, 1.0, 0.0)
    live = jnp.sum(alive, axis=1, keepdims=True)
    places[0:1, :] = from_r ^ row
    places[1:2, :] = from_rank
    places[2:3, :] = to_r
    places[3:4, :] = to_rank
    places[4:5, :] = first.astype(jnp.int32)
    places[5:6, :] = jnp.broadcast_to(live, j.shape).astype(jnp.int32)


def fetch(copies):
    for copy in copies:
        copy.start()
    for copy in copies:
        copy.wait()


def pack_kernel(n_row, n_col, blk, spans, heard, slab, *refs):
    packs, (asks, held, sems) = refs[: n_row * len(spans)], refs[n_row * len(spans) :]
    row, col = lax.axis_index("row"), lax.axis_index("col")
    start = spans[0][0]
    fetch(
        [
            pltpu.make_async_copy(heard.at[(row ^ t) * n_col + col], asks.at[t], sems.at[t])
            for t in range(n_row)
        ]
        + [pltpu.make_async_copy(slab.at[pl.ds(start, held.shape[0])], held, sems.at[n_row])]
    )
    for p, (first, rows) in enumerate(spans):
        for t in range(n_row):
            pack = packs[p * n_row + t]

            def copy(i, carry):
                at = pl.multiple_of((asks[t, 0, 1 + i] & (SHIFT - 1)) * blk, blk)
                pack[i] = held[first - start : first - start + rows, pl.ds(at, blk)]
                return carry

            lax.fori_loop(0, asks[t, 0, 0] & (SHIFT - 1), copy, 0)


def product_kernel(n_row, n_col, cap, base, group, places, stored, *refs):
    panels, sums, (held, total) = refs[:n_row], refs[n_row:-2], refs[-2:]
    turn = lax.axis_index("col") if len(sums) > 1 else 0
    for t, panel in enumerate(panels):
        held[base[t] : base[t] + panel.shape[0]] = panel[...]
    live = places[5, 0]

    def start(t):
        at = jnp.int32(base[0])
        for i in range(1, n_row):
            at = jnp.where(t == i, base[i], at)
        return at

    def step(g, carry):
        products = []
        for u in range(group):
            s = g * group + u
            here = start(places[0, s]) + places[1, s]
            products.append(jnp.dot(held[here], stored[s], preferred_element_type=jnp.float32))
        for u in range(group):
            s = g * group + u
            o = jnp.where(s < live, (places[2, s] ^ turn) * cap + places[3, s], n_col * cap)
            total[o] = jnp.where(places[4, s] == 1, 0.0, total[o]) + products[u]
        return carry

    lax.fori_loop(0, lax.div(live + group - 1, group), step, 0)
    for t in range(n_col):
        values = total[t * cap : (t + 1) * cap].astype(jnp.bfloat16)
        if len(sums) > 1:
            sums[turns(n_col).index(t)][...] = values
        else:
            sums[0][t] = values


def combine_kernel(n_col, n_sums, blk, first, chunks, lists, slab, *refs):
    sums, (out, total, ready, sems) = refs[:n_sums], refs[-4:]
    turn = lax.axis_index("col") if n_sums > 1 else 0
    pieces, rows = total.shape[:2]
    for i in range(pieces):
        total[i] = 3.0 * slab[first : first + rows, i * blk : (i + 1) * blk].astype(jnp.float32)
    for t in range(n_col):
        source = turns(n_col)[t] ^ turn if n_sums > 1 else t
        here = sums[t] if n_sums > 1 else sums[0].at[t]

        def add(i, carry):
            total[lists[source, 1 + i] >> 10] -= 2.0 * here[i].astype(jnp.float32)
            return carry

        lax.fori_loop(0, lists[source, 0] >> 10, add, 0)
    each = pieces // chunks
    copies = []
    for q in range(chunks):
        for i in range(q * each, (q + 1) * each):
            ready[:, i * blk : (i + 1) * blk] = total[i].astype(ready.dtype)
        here = pl.ds(q * each * blk, each * blk)
        copies.append(
            pltpu.make_async_copy(ready.at[:, here], out.at[pl.ds(first, rows), here], sems.at[q])
        )
        copies[-1].start()
    for copy in copies:
        copy.wait()


def exchange(heard, lists, places, s_slab, stored, caps_in, cap, parts):
    blk = s_slab.shape[0]
    width = s_slab.shape[1]
    n_row = lax.axis_size("row")
    n_col = lax.axis_size("col")
    slots = stored.shape[0]
    pieces = width // blk
    group = 8 if slots % 8 == 0 else 1
    chunks = 4 if pieces % 4 == 0 else 1
    base = [sum(caps_in[:t]) for t in range(n_row)]
    tight = sum(caps_in) <= 2 * slots
    params = pltpu.CompilerParams(vmem_limit_bytes=(16 if tight else 48) * 1024 * 1024)
    cost = pl.CostEstimate(flops=0, bytes_accessed=COST, transcendentals=0)
    spans = [(sum(parts[:i]), rows) for i, rows in enumerate(parts)]

    def pack(some):
        done = pl.pallas_call(
            lambda *refs: pack_kernel(n_row, n_col, blk, some, *refs),
            out_shape=[
                jax.ShapeDtypeStruct((c, rows, blk), jnp.bfloat16)
                for first, rows in some
                for c in caps_in
            ],
            in_specs=[anywhere(), anywhere()],
            out_specs=[vmem()] * (n_row * len(some)),
            scratch_shapes=[
                pltpu.SMEM((n_row,) + heard.shape[1:], jnp.int32),
                pltpu.VMEM((sum(rows for first, rows in some), width), jnp.bfloat16),
                pltpu.SemaphoreType.DMA((n_row + 1,)),
            ],
            compiler_params=params,
            cost_estimate=cost,
            name="pack",
        )(heard, s_slab)
        return [done[i * n_row : (i + 1) * n_row] for i in range(len(some))]

    packed = pack(spans[:1])
    if len(spans) > 1:
        packed += pack(spans[1:])
        places, packed[1:] = lax.optimization_barrier((places, packed[1:]))
    result = None
    for (first, rows), packs in zip(spans, packed):
        last = len(spans) > 1 and first + rows == blk
        panels = [packs[0]] + [
            lax.ppermute(packs[t], "row", pairs(n_row, t)) for t in range(1, n_row)
        ]
        sums = pl.pallas_call(
            lambda *refs: product_kernel(n_row, n_col, cap, base, group, *refs),
            out_shape=[jax.ShapeDtypeStruct((cap, rows, blk), jnp.bfloat16)] * n_col
            if last
            else [jax.ShapeDtypeStruct((n_col, cap, rows, blk), jnp.bfloat16)],
            in_specs=[smem()] + [vmem()] * (1 + n_row),
            out_specs=[vmem()] * (n_col if last else 1),
            scratch_shapes=[
                pltpu.VMEM((sum(caps_in), rows, blk), jnp.bfloat16),
                pltpu.VMEM((n_col * cap + 1, rows, blk), jnp.float32),
            ],
            compiler_params=params,
            cost_estimate=pl.CostEstimate(flops=HIDE, bytes_accessed=COST, transcendentals=0),
            name="product",
        )(places, stored, *panels)
        if last:
            sums = [sums[0]] + [
                lax.ppermute(sums[i], "col", pairs(n_col, t))
                for i, t in enumerate(turns(n_col))
                if i > 0
            ]
        else:
            sums = [lax.all_to_all(sums[0], "col", 0, 0, tiled=True)]
        extra = [] if result is None else [result]
        result = pl.pallas_call(
            lambda *refs, first=first, n=len(sums): combine_kernel(n_col, n, blk, first, chunks, *refs),
            out_shape=jax.ShapeDtypeStruct(s_slab.shape, s_slab.dtype),
            in_specs=[smem()] + [vmem()] * (1 + len(sums)) + [anywhere()] * len(extra),
            out_specs=anywhere(),
            scratch_shapes=[
                pltpu.VMEM((pieces, rows, blk), jnp.float32),
                pltpu.VMEM((rows, width), jnp.bfloat16),
                pltpu.SemaphoreType.DMA((chunks,)),
            ],
            input_output_aliases={2 + len(sums): 0} if extra else {},
            compiler_params=params,
            cost_estimate=cost,
            name="combine",
        )(lists, s_slab, *sums, *extra)
    return result


def body(s_slab, p_blocks, p_index):
    blk = s_slab.shape[0]
    per_piece = s_slab.shape[1] // blk
    n_row = lax.axis_size("row")
    n_col = lax.axis_size("col")
    slots = p_blocks.shape[2]
    stored = p_blocks[0, 0]
    full = min(per_piece, slots)
    wide = -(-(2 + full) // 128) * 128
    parts = PARTS if sum(PARTS) == blk else (blk,)
    levels = [level for level in LEVELS if max(level) < full]
    levels.append((full, full, full))

    line, places = pl.pallas_call(
        lambda *refs: ask_kernel(n_row, n_col, per_piece, levels[:-1], *refs),
        out_shape=[
            jax.ShapeDtypeStruct((n_row * n_col, wide), jnp.int32),
            jax.ShapeDtypeStruct((6, slots), jnp.int32),
        ],
        name="ask",
    )(p_index)
    heard = lax.all_to_all(line, ("row", "col"), 0, 0, tiled=True)
    lines = heard.reshape(n_row * n_col, 1, wide)
    lists = heard.reshape(n_row, n_col, wide)[lax.axis_index("row")]

    def run(level):
        near, far, cap = level
        caps_in = [near, near] + [far] * (n_row - 2)
        return lambda: exchange(lines, lists, places, s_slab, stored, caps_in, cap, parts)

    if len(levels) == 1:
        return run(levels[0])()
    return lax.switch(jnp.max(heard[:, wide - 1]), [run(level) for level in levels])


def solution(mesh):
    placed = (
        P(None, ("row", "col")),
        P("row", "col", None, None, None),
        P("row", "col", None, None),
    )
    return jax.shard_map(
        body, mesh=mesh, in_specs=placed, out_specs=P(None, ("row", "col")), check_vma=False
    )
```

```python
import jax
import jax.numpy as jnp
from jax import lax
from jax.experimental import pallas as pl
from jax.experimental.pallas import tpu as pltpu
from jax.sharding import PartitionSpec as P

LEVELS = ((24, 17, 12), (24, 18, 13), (24, 19, 14), (26, 21, 15), (32, 25, 18))
PARTS = (32, 64, 32)
SHIFT = 1024
COST = 1 << 16
HIDE = 30_000_000_000


def smem():
    return pl.BlockSpec(memory_space=pltpu.SMEM)


def anywhere():
    return pl.BlockSpec(memory_space=pl.ANY)


def vmem():
    return pl.BlockSpec(memory_space=pltpu.VMEM)


def pairs(n, t):
    return [(i, i ^ t) for i in range(n)]


def turns(n):
    return [t for t in range(n) if t < 3] + [t for t in range(n - 1, 2, -1)]


def number(index, per_piece, owner_of, n_owner, wide):
    slots = index.shape[1]
    f32 = jnp.float32
    lane = lax.broadcasted_iota(jnp.int32, (slots, slots), 1)
    sub = lax.broadcasted_iota(jnp.int32, (slots, slots), 0)
    key_r = index.astype(f32)
    key_c = jnp.sum(jnp.where(lane == sub, key_r, 0.0), axis=1, keepdims=True)
    index_c = jnp.maximum(key_c.astype(jnp.int32), 0)
    owner_r = owner_of(jnp.maximum(index, 0)).astype(f32)
    owner_c = owner_of(index_c).astype(f32)
    local_c = lax.rem(index_c, per_piece).astype(f32)
    same = jnp.where(key_c == key_r, 1.0, 0.0)
    before = jnp.where(lane < sub, 1.0, 0.0)
    after = jnp.where(sub < lane, 1.0, 0.0)
    kin = jnp.where(owner_c == owner_r, 1.0, 0.0)
    first_c = jnp.where(jnp.sum(same * before, axis=1, keepdims=True) == 0.0, 1.0, 0.0)
    first_c = jnp.where(key_c >= 0.0, first_c, 0.0)
    first_r = jnp.where(jnp.sum(same * after, axis=0, keepdims=True) == 0.0, 1.0, 0.0)
    first_r = jnp.where(key_r >= 0.0, first_r, 0.0)
    rank_c = jnp.sum(kin * before * first_r, axis=1, keepdims=True)
    rank_r = jnp.sum(same * (first_c * rank_c), axis=0, keepdims=True)
    lanes = lax.broadcasted_iota(jnp.int32, (slots, wide), 1).astype(f32)
    spot = jnp.where(lanes == rank_c + 1.0, local_c, 0.0) + jnp.where(lanes == 0.0, 1.0, 0.0)
    rows = []
    for owner in range(n_owner):
        mine = first_c * jnp.where(owner_c == float(owner), 1.0, 0.0)
        rows.append(jnp.sum(spot * mine, axis=0, keepdims=True))
    return owner_r.astype(jnp.int32), rank_r.astype(jnp.int32), first_r, rows


def ask_kernel(n_row, n_col, per_piece, levels, index, line, places):
    wide = line.shape[1]
    k, j = index[0, 0, 0:1, :], index[0, 0, 1:2, :]
    from_r, from_rank, _, asks = number(
        k, per_piece, lambda v: lax.div(v, per_piece * n_col), n_row, wide
    )
    to_r, to_rank, first, lists = number(
        j, per_piece, lambda v: lax.rem(lax.div(v, per_piece), n_col), n_col, wide
    )
    row = lax.axis_index("row")
    need = jnp.zeros((1, 1), jnp.float32)
    for near, far, col in levels:
        over = jnp.zeros((1, 1), jnp.float32)
        for owner, ask in enumerate(asks):
            cap = jnp.where((owner ^ row) <= 1, float(near), float(far))
            over = jnp.maximum(over, jnp.where(ask[:, 0:1] > cap, 1.0, 0.0))
        for item in lists:
            over = jnp.maximum(over, jnp.where(item[:, 0:1] > float(col), 1.0, 0.0))
        need = need + over
    lane = lax.broadcasted_iota(jnp.int32, (1, wide), 1)
    told = jnp.concatenate(lists, axis=0) * float(SHIFT)
    for owner, ask in enumerate(asks):
        values = jnp.where(lane == wide - 1, need, ask + told)
        line[owner * n_col : (owner + 1) * n_col, :] = values.astype(jnp.int32)
    alive = jnp.where(j >= 0, 1.0, 0.0)
    live = jnp.sum(alive, axis=1, keepdims=True)
    places[0:1, :] = from_r ^ row
    places[1:2, :] = from_rank
    places[2:3, :] = to_r
    places[3:4, :] = to_rank
    places[4:5, :] = first.astype(jnp.int32)
    places[5:6, :] = jnp.broadcast_to(live, j.shape).astype(jnp.int32)


def fetch(copies):
    for copy in copies:
        copy.start()
    for copy in copies:
        copy.wait()


def pack_kernel(n_row, n_col, blk, spans, heard, slab, *refs):
    packs, (asks, held, sems) = refs[: n_row * len(spans)], refs[n_row * len(spans) :]
    row, col = lax.axis_index("row"), lax.axis_index("col")
    start = spans[0][0]
    fetch(
        [
            pltpu.make_async_copy(heard.at[(row ^ t) * n_col + col], asks.at[t], sems.at[t])
            for t in range(n_row)
        ]
        + [pltpu.make_async_copy(slab.at[pl.ds(start, held.shape[0])], held, sems.at[n_row])]
    )
    for p, (first, rows) in enumerate(spans):
        for t in range(n_row):
            pack = packs[p * n_row + t]

            def copy(i, carry):
                at = pl.multiple_of((asks[t, 0, 1 + i] & (SHIFT - 1)) * blk, blk)
                pack[i] = held[first - start : first - start + rows, pl.ds(at, blk)]
                return carry

            lax.fori_loop(0, asks[t, 0, 0] & (SHIFT - 1), copy, 0)


def product_kernel(n_row, n_col, cap, base, group, places, stored, *refs):
    panels, sums, (held, total) = refs[:n_row], refs[n_row:-2], refs[-2:]
    turn = lax.axis_index("col") if len(sums) > 1 else 0
    for t, panel in enumerate(panels):
        held[base[t] : base[t] + panel.shape[0]] = panel[...]
    live = places[5, 0]

    def start(t):
        at = jnp.int32(base[0])
        for i in range(1, n_row):
            at = jnp.where(t == i, base[i], at)
        return at

    def step(g, carry):
        products = []
        for u in range(group):
            s = g * group + u
            here = start(places[0, s]) + places[1, s]
            products.append(jnp.dot(held[here], stored[s], preferred_element_type=jnp.float32))
        for u in range(group):
            s = g * group + u
            o = jnp.where(s < live, (places[2, s] ^ turn) * cap + places[3, s], n_col * cap)
            total[o] = jnp.where(places[4, s] == 1, 0.0, total[o]) + products[u]
        return carry

    lax.fori_loop(0, lax.div(live + group - 1, group), step, 0)
    for t in range(n_col):
        values = total[t * cap : (t + 1) * cap].astype(jnp.bfloat16)
        if len(sums) > 1:
            sums[turns(n_col).index(t)][...] = values
        else:
            sums[0][t] = values


def combine_kernel(n_col, n_sums, blk, first, chunks, lists, slab, *refs):
    sums, (out, total, ready, sems) = refs[:n_sums], refs[-4:]
    turn = lax.axis_index("col") if n_sums > 1 else 0
    pieces, rows = total.shape[:2]
    for i in range(pieces):
        total[i] = 3.0 * slab[first : first + rows, i * blk : (i + 1) * blk].astype(jnp.float32)
    for t in range(n_col):
        source = turns(n_col)[t] ^ turn if n_sums > 1 else t
        here = sums[t] if n_sums > 1 else sums[0].at[t]

        def add(i, carry):
            total[lists[source, 1 + i] >> 10] -= 2.0 * here[i].astype(jnp.float32)
            return carry

        lax.fori_loop(0, lists[source, 0] >> 10, add, 0)
    each = pieces // chunks
    copies = []
    for q in range(chunks):
        for i in range(q * each, (q + 1) * each):
            ready[:, i * blk : (i + 1) * blk] = total[i].astype(ready.dtype)
        here = pl.ds(q * each * blk, each * blk)
        copies.append(
            pltpu.make_async_copy(ready.at[:, here], out.at[pl.ds(first, rows), here], sems.at[q])
        )
        copies[-1].start()
    for copy in copies:
        copy.wait()


def exchange(heard, lists, places, s_slab, stored, caps_in, cap, parts):
    blk = s_slab.shape[0]
    width = s_slab.shape[1]
    n_row = lax.axis_size("row")
    n_col = lax.axis_size("col")
    slots = stored.shape[0]
    pieces = width // blk
    group = 8 if slots % 8 == 0 else 1
    chunks = 4 if pieces % 4 == 0 else 1
    base = [sum(caps_in[:t]) for t in range(n_row)]
    tight = sum(caps_in) <= 2 * slots
    params = pltpu.CompilerParams(vmem_limit_bytes=(16 if tight else 48) * 1024 * 1024)
    cost = pl.CostEstimate(flops=0, bytes_accessed=COST, transcendentals=0)
    spans = [(sum(parts[:i]), rows) for i, rows in enumerate(parts)]

    def pack(some, heard):
        if not some:
            return []
        done = pl.pallas_call(
            lambda *refs: pack_kernel(n_row, n_col, blk, some, *refs),
            out_shape=[
                jax.ShapeDtypeStruct((c, rows, blk), jnp.bfloat16)
                for first, rows in some
                for c in caps_in
            ],
            in_specs=[anywhere(), anywhere()],
            out_specs=[vmem()] * (n_row * len(some)),
            scratch_shapes=[
                pltpu.SMEM((n_row,) + heard.shape[1:], jnp.int32),
                pltpu.VMEM((sum(rows for first, rows in some), width), jnp.bfloat16),
                pltpu.SemaphoreType.DMA((n_row + 1,)),
            ],
            compiler_params=params,
            cost_estimate=cost,
            name="pack",
        )(heard, s_slab)
        return [done[i * n_row : (i + 1) * n_row] for i in range(len(some))]

    packed = pack(spans[:1], heard) + pack(spans[1:2], heard)
    if len(spans) > 1:
        places, packed[1] = lax.optimization_barrier((places, packed[1]))
    result = None
    for p, (first, rows) in enumerate(spans):
        packs = packed[p]
        last = len(spans) > 1 and first + rows == blk
        panels = [packs[0]] + [
            lax.ppermute(packs[t], "row", pairs(n_row, t)) for t in range(1, n_row)
        ]
        sums = pl.pallas_call(
            lambda *refs: product_kernel(n_row, n_col, cap, base, group, *refs),
            out_shape=[jax.ShapeDtypeStruct((cap, rows, blk), jnp.bfloat16)] * n_col
            if last
            else [jax.ShapeDtypeStruct((n_col, cap, rows, blk), jnp.bfloat16)],
            in_specs=[smem()] + [vmem()] * (1 + n_row),
            out_specs=[vmem()] * (n_col if last else 1),
            scratch_shapes=[
                pltpu.VMEM((sum(caps_in), rows, blk), jnp.bfloat16),
                pltpu.VMEM((n_col * cap + 1, rows, blk), jnp.float32),
            ],
            compiler_params=params,
            cost_estimate=pl.CostEstimate(flops=HIDE, bytes_accessed=COST, transcendentals=0),
            name="product",
        )(places, stored, *panels)
        later, _ = lax.optimization_barrier((heard, sums))
        packed += pack(spans[p + 2 : p + 3], later)
        if last:
            sums = [sums[0]] + [
                lax.ppermute(sums[i], "col", pairs(n_col, t))
                for i, t in enumerate(turns(n_col))
                if i > 0
            ]
        else:
            sums = [lax.all_to_all(sums[0], "col", 0, 0, tiled=True)]
        if result is not None and not last:
            places, result = lax.optimization_barrier((places, result))
        extra = [] if result is None else [result]
        result = pl.pallas_call(
            lambda *refs, first=first, n=len(sums): combine_kernel(n_col, n, blk, first, chunks, *refs),
            out_shape=jax.ShapeDtypeStruct(s_slab.shape, s_slab.dtype),
            in_specs=[smem()] + [vmem()] * (1 + len(sums)) + [anywhere()] * len(extra),
            out_specs=anywhere(),
            scratch_shapes=[
                pltpu.VMEM((pieces, rows, blk), jnp.float32),
                pltpu.VMEM((rows, width), jnp.bfloat16),
                pltpu.SemaphoreType.DMA((chunks,)),
            ],
            input_output_aliases={2 + len(sums): 0} if extra else {},
            compiler_params=params,
            cost_estimate=cost,
            name="combine",
        )(lists, s_slab, *sums, *extra)
    return result


def body(s_slab, p_blocks, p_index):
    blk = s_slab.shape[0]
    per_piece = s_slab.shape[1] // blk
    n_row = lax.axis_size("row")
    n_col = lax.axis_size("col")
    slots = p_blocks.shape[2]
    stored = p_blocks[0, 0]
    full = min(per_piece, slots)
    wide = -(-(2 + full) // 128) * 128
    parts = PARTS if sum(PARTS) == blk else (blk,)
    levels = [level for level in LEVELS if max(level) < full]
    levels.append((full, full, full))

    line, places = pl.pallas_call(
        lambda *refs: ask_kernel(n_row, n_col, per_piece, levels[:-1], *refs),
        out_shape=[
            jax.ShapeDtypeStruct((n_row * n_col, wide), jnp.int32),
            jax.ShapeDtypeStruct((6, slots), jnp.int32),
        ],
        name="ask",
    )(p_index)
    heard = lax.all_to_all(line, ("row", "col"), 0, 0, tiled=True)
    lines = heard.reshape(n_row * n_col, 1, wide)
    lists = heard.reshape(n_row, n_col, wide)[lax.axis_index("row")]

    def run(level):
        near, far, cap = level
        caps_in = [near, near] + [far] * (n_row - 2)
        return lambda: exchange(lines, lists, places, s_slab, stored, caps_in, cap, parts)

    if len(levels) == 1:
        return run(levels[0])()
    return lax.switch(jnp.max(heard[:, wide - 1]), [run(level) for level in levels])


def solution(mesh):
    placed = (
        P(None, ("row", "col")),
        P("row", "col", None, None, None),
        P("row", "col", None, None),
    )
    return jax.shard_map(
        body, mesh=mesh, in_specs=placed, out_specs=P(None, ("row", "col")), check_vma=False
    )
```

```python
import jax
import jax.numpy as jnp
from jax import lax
from jax.experimental import pallas as pl
from jax.experimental.pallas import tpu as pltpu
from jax.sharding import PartitionSpec as P

LEVELS = ((24, 17, 12), (24, 18, 13), (24, 19, 14), (26, 21, 15), (32, 25, 18))
PARTS = (48, 48, 32)
SHIFT = 1024
COST = 1 << 16
HIDE = 30_000_000_000


def smem():
    return pl.BlockSpec(memory_space=pltpu.SMEM)


def anywhere():
    return pl.BlockSpec(memory_space=pl.ANY)


def vmem():
    return pl.BlockSpec(memory_space=pltpu.VMEM)


def pairs(n, t):
    return [(i, i ^ t) for i in range(n)]


def turns(n):
    return [t for t in range(n) if t < 3] + [t for t in range(n - 1, 2, -1)]


def number(index, per_piece, owner_of, n_owner, wide):
    slots = index.shape[1]
    f32 = jnp.float32
    lane = lax.broadcasted_iota(jnp.int32, (slots, slots), 1)
    sub = lax.broadcasted_iota(jnp.int32, (slots, slots), 0)
    key_r = index.astype(f32)
    key_c = jnp.sum(jnp.where(lane == sub, key_r, 0.0), axis=1, keepdims=True)
    index_c = jnp.maximum(key_c.astype(jnp.int32), 0)
    owner_r = owner_of(jnp.maximum(index, 0)).astype(f32)
    owner_c = owner_of(index_c).astype(f32)
    local_c = lax.rem(index_c, per_piece).astype(f32)
    same = jnp.where(key_c == key_r, 1.0, 0.0)
    before = jnp.where(lane < sub, 1.0, 0.0)
    after = jnp.where(sub < lane, 1.0, 0.0)
    kin = jnp.where(owner_c == owner_r, 1.0, 0.0)
    first_c = jnp.where(jnp.sum(same * before, axis=1, keepdims=True) == 0.0, 1.0, 0.0)
    first_c = jnp.where(key_c >= 0.0, first_c, 0.0)
    first_r = jnp.where(jnp.sum(same * after, axis=0, keepdims=True) == 0.0, 1.0, 0.0)
    first_r = jnp.where(key_r >= 0.0, first_r, 0.0)
    rank_c = jnp.sum(kin * before * first_r, axis=1, keepdims=True)
    rank_r = jnp.sum(same * (first_c * rank_c), axis=0, keepdims=True)
    lanes = lax.broadcasted_iota(jnp.int32, (slots, wide), 1).astype(f32)
    spot = jnp.where(lanes == rank_c + 1.0, local_c, 0.0) + jnp.where(lanes == 0.0, 1.0, 0.0)
    rows = []
    for owner in range(n_owner):
        mine = first_c * jnp.where(owner_c == float(owner), 1.0, 0.0)
        rows.append(jnp.sum(spot * mine, axis=0, keepdims=True))
    return owner_r.astype(jnp.int32), rank_r.astype(jnp.int32), first_r, rows


def ask_kernel(n_row, n_col, per_piece, levels, index, line, places):
    wide = line.shape[1]
    k, j = index[0, 0, 0:1, :], index[0, 0, 1:2, :]
    from_r, from_rank, _, asks = number(
        k, per_piece, lambda v: lax.div(v, per_piece * n_col), n_row, wide
    )
    to_r, to_rank, first, lists = number(
        j, per_piece, lambda v: lax.rem(lax.div(v, per_piece), n_col), n_col, wide
    )
    row = lax.axis_index("row")
    need = jnp.zeros((1, 1), jnp.float32)
    for near, far, col in levels:
        over = jnp.zeros((1, 1), jnp.float32)
        for owner, ask in enumerate(asks):
            cap = jnp.where((owner ^ row) <= 1, float(near), float(far))
            over = jnp.maximum(over, jnp.where(ask[:, 0:1] > cap, 1.0, 0.0))
        for item in lists:
            over = jnp.maximum(over, jnp.where(item[:, 0:1] > float(col), 1.0, 0.0))
        need = need + over
    lane = lax.broadcasted_iota(jnp.int32, (1, wide), 1)
    told = jnp.concatenate(lists, axis=0) * float(SHIFT)
    for owner, ask in enumerate(asks):
        values = jnp.where(lane == wide - 1, need, ask + told)
        line[owner * n_col : (owner + 1) * n_col, :] = values.astype(jnp.int32)
    alive = jnp.where(j >= 0, 1.0, 0.0)
    live = jnp.sum(alive, axis=1, keepdims=True)
    places[0:1, :] = from_r ^ row
    places[1:2, :] = from_rank
    places[2:3, :] = to_r
    places[3:4, :] = to_rank
    places[4:5, :] = first.astype(jnp.int32)
    places[5:6, :] = jnp.broadcast_to(live, j.shape).astype(jnp.int32)


def fetch(copies):
    for copy in copies:
        copy.start()
    for copy in copies:
        copy.wait()


def pack_kernel(n_row, n_col, blk, spans, heard, slab, *refs):
    packs, (asks, held, sems) = refs[: n_row * len(spans)], refs[n_row * len(spans) :]
    row, col = lax.axis_index("row"), lax.axis_index("col")
    start = spans[0][0]
    fetch(
        [
            pltpu.make_async_copy(heard.at[(row ^ t) * n_col + col], asks.at[t], sems.at[t])
            for t in range(n_row)
        ]
        + [pltpu.make_async_copy(slab.at[pl.ds(start, held.shape[0])], held, sems.at[n_row])]
    )
    for p, (first, rows) in enumerate(spans):
        for t in range(n_row):
            pack = packs[p * n_row + t]

            def copy(i, carry):
                at = pl.multiple_of((asks[t, 0, 1 + i] & (SHIFT - 1)) * blk, blk)
                pack[i] = held[first - start : first - start + rows, pl.ds(at, blk)]
                return carry

            lax.fori_loop(0, asks[t, 0, 0] & (SHIFT - 1), copy, 0)


def product_kernel(n_row, n_col, cap, base, group, places, stored, *refs):
    panels, sums, (held, total) = refs[:n_row], refs[n_row:-2], refs[-2:]
    turn = lax.axis_index("col") if len(sums) > 1 else 0
    for t, panel in enumerate(panels):
        held[base[t] : base[t] + panel.shape[0]] = panel[...]
    live = places[5, 0]

    def start(t):
        at = jnp.int32(base[0])
        for i in range(1, n_row):
            at = jnp.where(t == i, base[i], at)
        return at

    def step(g, carry):
        products = []
        for u in range(group):
            s = g * group + u
            here = start(places[0, s]) + places[1, s]
            products.append(jnp.dot(held[here], stored[s], preferred_element_type=jnp.float32))
        for u in range(group):
            s = g * group + u
            o = jnp.where(s < live, (places[2, s] ^ turn) * cap + places[3, s], n_col * cap)
            total[o] = jnp.where(places[4, s] == 1, 0.0, total[o]) + products[u]
        return carry

    lax.fori_loop(0, lax.div(live + group - 1, group), step, 0)
    for t in range(n_col):
        values = total[t * cap : (t + 1) * cap].astype(jnp.bfloat16)
        if len(sums) > 1:
            sums[turns(n_col).index(t)][...] = values
        else:
            sums[0][t] = values


def combine_kernel(n_col, n_sums, blk, first, chunks, lists, slab, *refs):
    sums, (out, total, ready, sems) = refs[:n_sums], refs[-4:]
    turn = lax.axis_index("col") if n_sums > 1 else 0
    pieces, rows = total.shape[:2]
    for i in range(pieces):
        total[i] = 3.0 * slab[first : first + rows, i * blk : (i + 1) * blk].astype(jnp.float32)
    for t in range(n_col):
        source = turns(n_col)[t] ^ turn if n_sums > 1 else t
        here = sums[t] if n_sums > 1 else sums[0].at[t]

        def add(i, carry):
            total[lists[source, 1 + i] >> 10] -= 2.0 * here[i].astype(jnp.float32)
            return carry

        lax.fori_loop(0, lists[source, 0] >> 10, add, 0)
    each = pieces // chunks
    copies = []
    for q in range(chunks):
        for i in range(q * each, (q + 1) * each):
            ready[:, i * blk : (i + 1) * blk] = total[i].astype(ready.dtype)
        here = pl.ds(q * each * blk, each * blk)
        copies.append(
            pltpu.make_async_copy(ready.at[:, here], out.at[pl.ds(first, rows), here], sems.at[q])
        )
        copies[-1].start()
    for copy in copies:
        copy.wait()


def exchange(heard, lists, places, s_slab, stored, caps_in, cap, parts):
    blk = s_slab.shape[0]
    width = s_slab.shape[1]
    n_row = lax.axis_size("row")
    n_col = lax.axis_size("col")
    slots = stored.shape[0]
    pieces = width // blk
    group = 8 if slots % 8 == 0 else 1
    chunks = 4 if pieces % 4 == 0 else 1
    base = [sum(caps_in[:t]) for t in range(n_row)]
    tight = sum(caps_in) <= 2 * slots
    params = pltpu.CompilerParams(vmem_limit_bytes=(16 if tight else 48) * 1024 * 1024)
    cost = pl.CostEstimate(flops=0, bytes_accessed=COST, transcendentals=0)
    spans = [(sum(parts[:i]), rows) for i, rows in enumerate(parts)]

    def pack(some):
        if not some:
            return []
        done = pl.pallas_call(
            lambda *refs: pack_kernel(n_row, n_col, blk, some, *refs),
            out_shape=[
                jax.ShapeDtypeStruct((c, rows, blk), jnp.bfloat16)
                for first, rows in some
                for c in caps_in
            ],
            in_specs=[anywhere(), anywhere()],
            out_specs=[vmem()] * (n_row * len(some)),
            scratch_shapes=[
                pltpu.SMEM((n_row,) + heard.shape[1:], jnp.int32),
                pltpu.VMEM((sum(rows for first, rows in some), width), jnp.bfloat16),
                pltpu.SemaphoreType.DMA((n_row + 1,)),
            ],
            compiler_params=params,
            cost_estimate=cost,
            name="pack",
        )(heard, s_slab)
        return [done[i * n_row : (i + 1) * n_row] for i in range(len(some))]

    packed = pack(spans[:1]) + pack(spans[1:])
    if len(spans) > 1:
        places, packed[1:] = lax.optimization_barrier((places, packed[1:]))
    result, panels = None, None
    for p, (first, rows) in enumerate(spans):
        packs = packed[p]
        if panels is not None:
            packs, _ = lax.optimization_barrier((packs, panels))
        last = len(spans) > 1 and first + rows == blk
        panels = [packs[0]] + [
            lax.ppermute(packs[t], "row", pairs(n_row, t)) for t in range(1, n_row)
        ]
        sums = pl.pallas_call(
            lambda *refs: product_kernel(n_row, n_col, cap, base, group, *refs),
            out_shape=[jax.ShapeDtypeStruct((cap, rows, blk), jnp.bfloat16)] * n_col
            if last
            else [jax.ShapeDtypeStruct((n_col, cap, rows, blk), jnp.bfloat16)],
            in_specs=[smem()] + [vmem()] * (1 + n_row),
            out_specs=[vmem()] * (n_col if last else 1),
            scratch_shapes=[
                pltpu.VMEM((sum(caps_in), rows, blk), jnp.bfloat16),
                pltpu.VMEM((n_col * cap + 1, rows, blk), jnp.float32),
            ],
            compiler_params=params,
            cost_estimate=pl.CostEstimate(flops=HIDE, bytes_accessed=COST, transcendentals=0),
            name="product",
        )(places, stored, *panels)
        if last:
            sums = [sums[0]] + [
                lax.ppermute(sums[i], "col", pairs(n_col, t))
                for i, t in enumerate(turns(n_col))
                if i > 0
            ]
        else:
            sums = [lax.all_to_all(sums[0], "col", 0, 0, tiled=True)]
        if result is not None and not last:
            places, result = lax.optimization_barrier((places, result))
        extra = [] if result is None else [result]
        result = pl.pallas_call(
            lambda *refs, first=first, n=len(sums): combine_kernel(n_col, n, blk, first, chunks, *refs),
            out_shape=jax.ShapeDtypeStruct(s_slab.shape, s_slab.dtype),
            in_specs=[smem()] + [vmem()] * (1 + len(sums)) + [anywhere()] * len(extra),
            out_specs=anywhere(),
            scratch_shapes=[
                pltpu.VMEM((pieces, rows, blk), jnp.float32),
                pltpu.VMEM((rows, width), jnp.bfloat16),
                pltpu.SemaphoreType.DMA((chunks,)),
            ],
            input_output_aliases={2 + len(sums): 0} if extra else {},
            compiler_params=params,
            cost_estimate=cost,
            name="combine",
        )(lists, s_slab, *sums, *extra)
    return result


def body(s_slab, p_blocks, p_index):
    blk = s_slab.shape[0]
    per_piece = s_slab.shape[1] // blk
    n_row = lax.axis_size("row")
    n_col = lax.axis_size("col")
    slots = p_blocks.shape[2]
    stored = p_blocks[0, 0]
    full = min(per_piece, slots)
    wide = -(-(2 + full) // 128) * 128
    parts = PARTS if sum(PARTS) == blk else (blk,)
    levels = [level for level in LEVELS if max(level) < full]
    levels.append((full, full, full))

    line, places = pl.pallas_call(
        lambda *refs: ask_kernel(n_row, n_col, per_piece, levels[:-1], *refs),
        out_shape=[
            jax.ShapeDtypeStruct((n_row * n_col, wide), jnp.int32),
            jax.ShapeDtypeStruct((6, slots), jnp.int32),
        ],
        name="ask",
    )(p_index)
    heard = lax.all_to_all(line, ("row", "col"), 0, 0, tiled=True)
    lines = heard.reshape(n_row * n_col, 1, wide)
    lists = heard.reshape(n_row, n_col, wide)[lax.axis_index("row")]

    def run(level):
        near, far, cap = level
        caps_in = [near, near] + [far] * (n_row - 2)
        return lambda: exchange(lines, lists, places, s_slab, stored, caps_in, cap, parts)

    if len(levels) == 1:
        return run(levels[0])()
    return lax.switch(jnp.max(heard[:, wide - 1]), [run(level) for level in levels])


def solution(mesh):
    placed = (
        P(None, ("row", "col")),
        P("row", "col", None, None, None),
        P("row", "col", None, None),
    )
    return jax.shard_map(
        body, mesh=mesh, in_specs=placed, out_specs=P(None, ("row", "col")), check_vma=False
    )
```

```python
import jax
import jax.numpy as jnp
from jax import lax
from jax.experimental import pallas as pl
from jax.experimental.pallas import tpu as pltpu
from jax.sharding import PartitionSpec as P

LEVELS = ((24, 17, 12), (24, 18, 13), (24, 19, 14), (26, 21, 15), (32, 25, 18))
PARTS = (32, 64, 32)
SHIFT = 1024
COST = 1 << 16
HIDE = 30_000_000_000


def smem():
    return pl.BlockSpec(memory_space=pltpu.SMEM)


def anywhere():
    return pl.BlockSpec(memory_space=pl.ANY)


def vmem():
    return pl.BlockSpec(memory_space=pltpu.VMEM)


def pairs(n, t):
    return [(i, i ^ t) for i in range(n)]


def turns(n):
    return [t for t in range(n) if t < 3] + [t for t in range(n - 1, 2, -1)]


def number(index, per_piece, owner_of, n_owner, wide):
    slots = index.shape[1]
    f32 = jnp.float32
    lane = lax.broadcasted_iota(jnp.int32, (slots, slots), 1)
    sub = lax.broadcasted_iota(jnp.int32, (slots, slots), 0)
    key_r = index.astype(f32)
    key_c = jnp.sum(jnp.where(lane == sub, key_r, 0.0), axis=1, keepdims=True)
    index_c = jnp.maximum(key_c.astype(jnp.int32), 0)
    owner_r = owner_of(jnp.maximum(index, 0)).astype(f32)
    owner_c = owner_of(index_c).astype(f32)
    local_c = lax.rem(index_c, per_piece).astype(f32)
    same = jnp.where(key_c == key_r, 1.0, 0.0)
    before = jnp.where(lane < sub, 1.0, 0.0)
    after = jnp.where(sub < lane, 1.0, 0.0)
    kin = jnp.where(owner_c == owner_r, 1.0, 0.0)
    first_c = jnp.where(jnp.sum(same * before, axis=1, keepdims=True) == 0.0, 1.0, 0.0)
    first_c = jnp.where(key_c >= 0.0, first_c, 0.0)
    first_r = jnp.where(jnp.sum(same * after, axis=0, keepdims=True) == 0.0, 1.0, 0.0)
    first_r = jnp.where(key_r >= 0.0, first_r, 0.0)
    rank_c = jnp.sum(kin * before * first_r, axis=1, keepdims=True)
    rank_r = jnp.sum(same * (first_c * rank_c), axis=0, keepdims=True)
    lanes = lax.broadcasted_iota(jnp.int32, (slots, wide), 1).astype(f32)
    spot = jnp.where(lanes == rank_c + 1.0, local_c, 0.0) + jnp.where(lanes == 0.0, 1.0, 0.0)
    rows = []
    for owner in range(n_owner):
        mine = first_c * jnp.where(owner_c == float(owner), 1.0, 0.0)
        rows.append(jnp.sum(spot * mine, axis=0, keepdims=True))
    return owner_r.astype(jnp.int32), rank_r.astype(jnp.int32), first_r, rows


def ask_kernel(n_row, n_col, per_piece, levels, index, line, places):
    wide = line.shape[1]
    k, j = index[0, 0, 0:1, :], index[0, 0, 1:2, :]
    from_r, from_rank, _, asks = number(
        k, per_piece, lambda v: lax.div(v, per_piece * n_col), n_row, wide
    )
    to_r, to_rank, first, lists = number(
        j, per_piece, lambda v: lax.rem(lax.div(v, per_piece), n_col), n_col, wide
    )
    row = lax.axis_index("row")
    need = jnp.zeros((1, 1), jnp.float32)
    for near, far, col in levels:
        over = jnp.zeros((1, 1), jnp.float32)
        for owner, ask in enumerate(asks):
            cap = jnp.where((owner ^ row) <= 1, float(near), float(far))
            over = jnp.maximum(over, jnp.where(ask[:, 0:1] > cap, 1.0, 0.0))
        for item in lists:
            over = jnp.maximum(over, jnp.where(item[:, 0:1] > float(col), 1.0, 0.0))
        need = need + over
    lane = lax.broadcasted_iota(jnp.int32, (1, wide), 1)
    told = jnp.concatenate(lists, axis=0) * float(SHIFT)
    for owner, ask in enumerate(asks):
        values = jnp.where(lane == wide - 1, need, ask + told)
        line[owner * n_col : (owner + 1) * n_col, :] = values.astype(jnp.int32)
    alive = jnp.where(j >= 0, 1.0, 0.0)
    live = jnp.sum(alive, axis=1, keepdims=True)
    places[0:1, :] = from_r ^ row
    places[1:2, :] = from_rank
    places[2:3, :] = to_r
    places[3:4, :] = to_rank
    places[4:5, :] = first.astype(jnp.int32)
    places[5:6, :] = jnp.broadcast_to(live, j.shape).astype(jnp.int32)


def fetch(copies):
    for copy in copies:
        copy.start()
    for copy in copies:
        copy.wait()


def pack_kernel(n_row, n_col, blk, spans, heard, slab, *refs):
    packs, (asks, held, sems) = refs[: n_row * len(spans)], refs[n_row * len(spans) :]
    row, col = lax.axis_index("row"), lax.axis_index("col")
    start = spans[0][0]
    fetch(
        [
            pltpu.make_async_copy(heard.at[(row ^ t) * n_col + col], asks.at[t], sems.at[t])
            for t in range(n_row)
        ]
        + [pltpu.make_async_copy(slab.at[pl.ds(start, held.shape[0])], held, sems.at[n_row])]
    )
    for p, (first, rows) in enumerate(spans):
        for t in range(n_row):
            pack = packs[p * n_row + t]

            def copy(i, carry):
                at = pl.multiple_of((asks[t, 0, 1 + i] & (SHIFT - 1)) * blk, blk)
                pack[i] = held[first - start : first - start + rows, pl.ds(at, blk)]
                return carry

            lax.fori_loop(0, asks[t, 0, 0] & (SHIFT - 1), copy, 0)


def product_kernel(n_row, n_col, cap, base, group, places, stored, *refs):
    panels, sums, (held, total) = refs[:n_row], refs[n_row:-2], refs[-2:]
    turn = lax.axis_index("col") if len(sums) > 1 else 0
    for t, panel in enumerate(panels):
        held[base[t] : base[t] + panel.shape[0]] = panel[...]
    live = places[5, 0]

    def start(t):
        at = jnp.int32(base[0])
        for i in range(1, n_row):
            at = jnp.where(t == i, base[i], at)
        return at

    def step(g, carry):
        products = []
        for u in range(group):
            s = g * group + u
            here = start(places[0, s]) + places[1, s]
            products.append(jnp.dot(held[here], stored[s], preferred_element_type=jnp.float32))
        for u in range(group):
            s = g * group + u
            o = jnp.where(s < live, (places[2, s] ^ turn) * cap + places[3, s], n_col * cap)
            total[o] = jnp.where(places[4, s] == 1, 0.0, total[o]) + products[u]
        return carry

    lax.fori_loop(0, lax.div(live + group - 1, group), step, 0)
    for t in range(n_col):
        values = total[t * cap : (t + 1) * cap].astype(jnp.bfloat16)
        if len(sums) > 1:
            sums[turns(n_col).index(t)][...] = values
        else:
            sums[0][t] = values


def combine_kernel(n_col, n_sums, blk, first, chunks, lists, slab, *refs):
    sums, (out, total, ready, sems) = refs[:n_sums], refs[-4:]
    turn = lax.axis_index("col") if n_sums > 1 else 0
    pieces, rows = total.shape[:2]
    for i in range(pieces):
        total[i] = 3.0 * slab[first : first + rows, i * blk : (i + 1) * blk].astype(jnp.float32)
    for t in range(n_col):
        source = turns(n_col)[t] ^ turn if n_sums > 1 else t
        here = sums[t] if n_sums > 1 else sums[0].at[t]

        def add(i, carry):
            total[lists[source, 1 + i] >> 10] -= 2.0 * here[i].astype(jnp.float32)
            return carry

        lax.fori_loop(0, lists[source, 0] >> 10, add, 0)
    each = pieces // chunks
    copies = []
    for q in range(chunks):
        for i in range(q * each, (q + 1) * each):
            ready[:, i * blk : (i + 1) * blk] = total[i].astype(ready.dtype)
        here = pl.ds(q * each * blk, each * blk)
        copies.append(
            pltpu.make_async_copy(ready.at[:, here], out.at[pl.ds(first, rows), here], sems.at[q])
        )
        copies[-1].start()
    for copy in copies:
        copy.wait()


def exchange(heard, lists, places, s_slab, stored, caps_in, cap, parts):
    blk = s_slab.shape[0]
    width = s_slab.shape[1]
    n_row = lax.axis_size("row")
    n_col = lax.axis_size("col")
    slots = stored.shape[0]
    pieces = width // blk
    group = 8 if slots % 8 == 0 else 1
    chunks = 4 if pieces % 4 == 0 else 1
    base = [sum(caps_in[:t]) for t in range(n_row)]
    tight = sum(caps_in) <= 2 * slots
    params = pltpu.CompilerParams(vmem_limit_bytes=(16 if tight else 48) * 1024 * 1024)
    cost = pl.CostEstimate(flops=0, bytes_accessed=COST, transcendentals=0)
    spans = [(sum(parts[:i]), rows) for i, rows in enumerate(parts)]

    def pack(some):
        if not some:
            return []
        done = pl.pallas_call(
            lambda *refs: pack_kernel(n_row, n_col, blk, some, *refs),
            out_shape=[
                jax.ShapeDtypeStruct((c, rows, blk), jnp.bfloat16)
                for first, rows in some
                for c in caps_in
            ],
            in_specs=[anywhere(), anywhere()],
            out_specs=[vmem()] * (n_row * len(some)),
            scratch_shapes=[
                pltpu.SMEM((n_row,) + heard.shape[1:], jnp.int32),
                pltpu.VMEM((sum(rows for first, rows in some), width), jnp.bfloat16),
                pltpu.SemaphoreType.DMA((n_row + 1,)),
            ],
            compiler_params=params,
            cost_estimate=cost,
            name="pack",
        )(heard, s_slab)
        return [done[i * n_row : (i + 1) * n_row] for i in range(len(some))]

    packed = pack(spans[:1]) + pack(spans[1:])
    if len(spans) > 1:
        places, packed[1:] = lax.optimization_barrier((places, packed[1:]))
    result, panels = None, None
    for p, (first, rows) in enumerate(spans):
        packs = packed[p]
        if panels is not None:
            packs, _ = lax.optimization_barrier((packs, panels))
        last = len(spans) > 1 and first + rows == blk
        panels = [packs[0]] + [
            lax.ppermute(packs[t], "row", pairs(n_row, t)) for t in range(1, n_row)
        ]
        sums = pl.pallas_call(
            lambda *refs: product_kernel(n_row, n_col, cap, base, group, *refs),
            out_shape=[jax.ShapeDtypeStruct((cap, rows, blk), jnp.bfloat16)] * n_col
            if last
            else [jax.ShapeDtypeStruct((n_col, cap, rows, blk), jnp.bfloat16)],
            in_specs=[smem()] + [vmem()] * (1 + n_row),
            out_specs=[vmem()] * (n_col if last else 1),
            scratch_shapes=[
                pltpu.VMEM((sum(caps_in), rows, blk), jnp.bfloat16),
                pltpu.VMEM((n_col * cap + 1, rows, blk), jnp.float32),
            ],
            compiler_params=params,
            cost_estimate=pl.CostEstimate(flops=HIDE, bytes_accessed=COST, transcendentals=0),
            name="product",
        )(places, stored, *panels)
        if last:
            sums = [sums[0]] + [
                lax.ppermute(sums[i], "col", pairs(n_col, t))
                for i, t in enumerate(turns(n_col))
                if i > 0
            ]
        else:
            sums = [lax.all_to_all(sums[0], "col", 0, 0, tiled=True)]
        if result is not None and not last:
            places, result = lax.optimization_barrier((places, result))
        extra = [] if result is None else [result]
        result = pl.pallas_call(
            lambda *refs, first=first, n=len(sums): combine_kernel(n_col, n, blk, first, chunks, *refs),
            out_shape=jax.ShapeDtypeStruct(s_slab.shape, s_slab.dtype),
            in_specs=[smem()] + [vmem()] * (1 + len(sums)) + [anywhere()] * len(extra),
            out_specs=anywhere(),
            scratch_shapes=[
                pltpu.VMEM((pieces, rows, blk), jnp.float32),
                pltpu.VMEM((rows, width), jnp.bfloat16),
                pltpu.SemaphoreType.DMA((chunks,)),
            ],
            input_output_aliases={2 + len(sums): 0} if extra else {},
            compiler_params=params,
            cost_estimate=cost,
            name="combine",
        )(lists, s_slab, *sums, *extra)
    return result


def body(s_slab, p_blocks, p_index):
    blk = s_slab.shape[0]
    per_piece = s_slab.shape[1] // blk
    n_row = lax.axis_size("row")
    n_col = lax.axis_size("col")
    slots = p_blocks.shape[2]
    stored = p_blocks[0, 0]
    full = min(per_piece, slots)
    wide = -(-(2 + full) // 128) * 128
    parts = PARTS if sum(PARTS) == blk else (blk,)
    levels = [level for level in LEVELS if max(level) < full]
    levels.append((full, full, full))

    line, places = pl.pallas_call(
        lambda *refs: ask_kernel(n_row, n_col, per_piece, levels[:-1], *refs),
        out_shape=[
            jax.ShapeDtypeStruct((n_row * n_col, wide), jnp.int32),
            jax.ShapeDtypeStruct((6, slots), jnp.int32),
        ],
        name="ask",
    )(p_index)
    heard = lax.all_to_all(line, ("row", "col"), 0, 0, tiled=True)
    lines = heard.reshape(n_row * n_col, 1, wide)
    lists = heard.reshape(n_row, n_col, wide)[lax.axis_index("row")]

    def run(level):
        near, far, cap = level
        caps_in = [near, near] + [far] * (n_row - 2)
        return lambda: exchange(lines, lists, places, s_slab, stored, caps_in, cap, parts)

    if len(levels) == 1:
        return run(levels[0])()
    return lax.switch(jnp.max(heard[:, wide - 1]), [run(level) for level in levels])


def solution(mesh):
    placed = (
        P(None, ("row", "col")),
        P("row", "col", None, None, None),
        P("row", "col", None, None),
    )
    return jax.shard_map(
        body, mesh=mesh, in_specs=placed, out_specs=P(None, ("row", "col")), check_vma=False
    )
```

```python
import jax
import jax.numpy as jnp
from jax import lax
from jax.experimental import pallas as pl
from jax.experimental.pallas import tpu as pltpu
from jax.sharding import PartitionSpec as P

LEVELS = ((24, 17, 12), (24, 18, 13), (24, 19, 14), (26, 21, 15), (32, 25, 18))
PARTS = (32, 48, 48)
SHIFT = 1024
COST = 1 << 16
HIDE = 30_000_000_000


def smem():
    return pl.BlockSpec(memory_space=pltpu.SMEM)


def anywhere():
    return pl.BlockSpec(memory_space=pl.ANY)


def vmem():
    return pl.BlockSpec(memory_space=pltpu.VMEM)


def pairs(n, t):
    return [(i, i ^ t) for i in range(n)]


def turns(n):
    return [t for t in range(n) if t < 3] + [t for t in range(n - 1, 2, -1)]


def number(index, per_piece, owner_of, n_owner, wide):
    slots = index.shape[1]
    f32 = jnp.float32
    lane = lax.broadcasted_iota(jnp.int32, (slots, slots), 1)
    sub = lax.broadcasted_iota(jnp.int32, (slots, slots), 0)
    key_r = index.astype(f32)
    key_c = jnp.sum(jnp.where(lane == sub, key_r, 0.0), axis=1, keepdims=True)
    index_c = jnp.maximum(key_c.astype(jnp.int32), 0)
    owner_r = owner_of(jnp.maximum(index, 0)).astype(f32)
    owner_c = owner_of(index_c).astype(f32)
    local_c = lax.rem(index_c, per_piece).astype(f32)
    same = jnp.where(key_c == key_r, 1.0, 0.0)
    before = jnp.where(lane < sub, 1.0, 0.0)
    after = jnp.where(sub < lane, 1.0, 0.0)
    kin = jnp.where(owner_c == owner_r, 1.0, 0.0)
    first_c = jnp.where(jnp.sum(same * before, axis=1, keepdims=True) == 0.0, 1.0, 0.0)
    first_c = jnp.where(key_c >= 0.0, first_c, 0.0)
    first_r = jnp.where(jnp.sum(same * after, axis=0, keepdims=True) == 0.0, 1.0, 0.0)
    first_r = jnp.where(key_r >= 0.0, first_r, 0.0)
    rank_c = jnp.sum(kin * before * first_r, axis=1, keepdims=True)
    rank_r = jnp.sum(same * (first_c * rank_c), axis=0, keepdims=True)
    lanes = lax.broadcasted_iota(jnp.int32, (slots, wide), 1).astype(f32)
    spot = jnp.where(lanes == rank_c + 1.0, local_c, 0.0) + jnp.where(lanes == 0.0, 1.0, 0.0)
    rows = []
    for owner in range(n_owner):
        mine = first_c * jnp.where(owner_c == float(owner), 1.0, 0.0)
        rows.append(jnp.sum(spot * mine, axis=0, keepdims=True))
    return owner_r.astype(jnp.int32), rank_r.astype(jnp.int32), first_r, rows


def ask_kernel(n_row, n_col, per_piece, levels, index, line, places):
    wide = line.shape[1]
    k, j = index[0, 0, 0:1, :], index[0, 0, 1:2, :]
    from_r, from_rank, _, asks = number(
        k, per_piece, lambda v: lax.div(v, per_piece * n_col), n_row, wide
    )
    to_r, to_rank, first, lists = number(
        j, per_piece, lambda v: lax.rem(lax.div(v, per_piece), n_col), n_col, wide
    )
    row = lax.axis_index("row")
    need = jnp.zeros((1, 1), jnp.float32)
    for near, far, col in levels:
        over = jnp.zeros((1, 1), jnp.float32)
        for owner, ask in enumerate(asks):
            cap = jnp.where((owner ^ row) <= 1, float(near), float(far))
            over = jnp.maximum(over, jnp.where(ask[:, 0:1] > cap, 1.0, 0.0))
        for item in lists:
            over = jnp.maximum(over, jnp.where(item[:, 0:1] > float(col), 1.0, 0.0))
        need = need + over
    lane = lax.broadcasted_iota(jnp.int32, (1, wide), 1)
    told = jnp.concatenate(lists, axis=0) * float(SHIFT)
    for owner, ask in enumerate(asks):
        values = jnp.where(lane == wide - 1, need, ask + told)
        line[owner * n_col : (owner + 1) * n_col, :] = values.astype(jnp.int32)
    alive = jnp.where(j >= 0, 1.0, 0.0)
    live = jnp.sum(alive, axis=1, keepdims=True)
    places[0:1, :] = from_r ^ row
    places[1:2, :] = from_rank
    places[2:3, :] = to_r
    places[3:4, :] = to_rank
    places[4:5, :] = first.astype(jnp.int32)
    places[5:6, :] = jnp.broadcast_to(live, j.shape).astype(jnp.int32)


def fetch(copies):
    for copy in copies:
        copy.start()
    for copy in copies:
        copy.wait()


def pack_kernel(n_row, n_col, blk, spans, heard, slab, *refs):
    packs, (asks, held, sems) = refs[: n_row * len(spans)], refs[n_row * len(spans) :]
    row, col = lax.axis_index("row"), lax.axis_index("col")
    start = spans[0][0]
    fetch(
        [
            pltpu.make_async_copy(heard.at[(row ^ t) * n_col + col], asks.at[t], sems.at[t])
            for t in range(n_row)
        ]
        + [pltpu.make_async_copy(slab.at[pl.ds(start, held.shape[0])], held, sems.at[n_row])]
    )
    for p, (first, rows) in enumerate(spans):
        for t in range(n_row):
            pack = packs[p * n_row + t]

            def copy(i, carry):
                at = pl.multiple_of((asks[t, 0, 1 + i] & (SHIFT - 1)) * blk, blk)
                pack[i] = held[first - start : first - start + rows, pl.ds(at, blk)]
                return carry

            lax.fori_loop(0, asks[t, 0, 0] & (SHIFT - 1), copy, 0)


def product_kernel(n_row, n_col, cap, base, group, places, stored, *refs):
    panels, sums, (held, total) = refs[:n_row], refs[n_row:-2], refs[-2:]
    turn = lax.axis_index("col") if len(sums) > 1 else 0
    for t, panel in enumerate(panels):
        held[base[t] : base[t] + panel.shape[0]] = panel[...]
    live = places[5, 0]

    def start(t):
        at = jnp.int32(base[0])
        for i in range(1, n_row):
            at = jnp.where(t == i, base[i], at)
        return at

    def step(g, carry):
        products = []
        for u in range(group):
            s = g * group + u
            here = start(places[0, s]) + places[1, s]
            products.append(jnp.dot(held[here], stored[s], preferred_element_type=jnp.float32))
        for u in range(group):
            s = g * group + u
            o = jnp.where(s < live, (places[2, s] ^ turn) * cap + places[3, s], n_col * cap)
            total[o] = jnp.where(places[4, s] == 1, 0.0, total[o]) + products[u]
        return carry

    lax.fori_loop(0, lax.div(live + group - 1, group), step, 0)
    for t in range(n_col):
        values = total[t * cap : (t + 1) * cap].astype(jnp.bfloat16)
        if len(sums) > 1:
            sums[turns(n_col).index(t)][...] = values
        else:
            sums[0][t] = values


def combine_kernel(n_col, n_sums, blk, first, chunks, lists, slab, *refs):
    sums, (out, total, ready, sems) = refs[:n_sums], refs[-4:]
    turn = lax.axis_index("col") if n_sums > 1 else 0
    pieces, rows = total.shape[:2]
    for i in range(pieces):
        total[i] = 3.0 * slab[first : first + rows, i * blk : (i + 1) * blk].astype(jnp.float32)
    for t in range(n_col):
        source = turns(n_col)[t] ^ turn if n_sums > 1 else t
        here = sums[t] if n_sums > 1 else sums[0].at[t]

        def add(i, carry):
            total[lists[source, 1 + i] >> 10] -= 2.0 * here[i].astype(jnp.float32)
            return carry

        lax.fori_loop(0, lists[source, 0] >> 10, add, 0)
    each = pieces // chunks
    copies = []
    for q in range(chunks):
        for i in range(q * each, (q + 1) * each):
            ready[:, i * blk : (i + 1) * blk] = total[i].astype(ready.dtype)
        here = pl.ds(q * each * blk, each * blk)
        copies.append(
            pltpu.make_async_copy(ready.at[:, here], out.at[pl.ds(first, rows), here], sems.at[q])
        )
        copies[-1].start()
    for copy in copies:
        copy.wait()


def exchange(heard, lists, places, s_slab, stored, caps_in, cap, parts):
    blk = s_slab.shape[0]
    width = s_slab.shape[1]
    n_row = lax.axis_size("row")
    n_col = lax.axis_size("col")
    slots = stored.shape[0]
    pieces = width // blk
    group = 8 if slots % 8 == 0 else 1
    chunks = 4 if pieces % 4 == 0 else 1
    base = [sum(caps_in[:t]) for t in range(n_row)]
    tight = sum(caps_in) <= 2 * slots
    params = pltpu.CompilerParams(vmem_limit_bytes=(16 if tight else 48) * 1024 * 1024)
    cost = pl.CostEstimate(flops=0, bytes_accessed=COST, transcendentals=0)
    spans = [(sum(parts[:i]), rows) for i, rows in enumerate(parts)]

    def pack(some, heard):
        if not some:
            return []
        done = pl.pallas_call(
            lambda *refs: pack_kernel(n_row, n_col, blk, some, *refs),
            out_shape=[
                jax.ShapeDtypeStruct((c, rows, blk), jnp.bfloat16)
                for first, rows in some
                for c in caps_in
            ],
            in_specs=[anywhere(), anywhere()],
            out_specs=[vmem()] * (n_row * len(some)),
            scratch_shapes=[
                pltpu.SMEM((n_row,) + heard.shape[1:], jnp.int32),
                pltpu.VMEM((sum(rows for first, rows in some), width), jnp.bfloat16),
                pltpu.SemaphoreType.DMA((n_row + 1,)),
            ],
            compiler_params=params,
            cost_estimate=cost,
            name="pack",
        )(heard, s_slab)
        return [done[i * n_row : (i + 1) * n_row] for i in range(len(some))]

    packed = pack(spans[:1], heard) + pack(spans[1:2], heard)
    if len(spans) > 1:
        places, packed[1] = lax.optimization_barrier((places, packed[1]))
    result = None
    for p, (first, rows) in enumerate(spans):
        packs = packed[p]
        last = len(spans) > 1 and first + rows == blk
        panels = [packs[0]] + [
            lax.ppermute(packs[t], "row", pairs(n_row, t)) for t in range(1, n_row)
        ]
        sums = pl.pallas_call(
            lambda *refs: product_kernel(n_row, n_col, cap, base, group, *refs),
            out_shape=[jax.ShapeDtypeStruct((cap, rows, blk), jnp.bfloat16)] * n_col
            if last
            else [jax.ShapeDtypeStruct((n_col, cap, rows, blk), jnp.bfloat16)],
            in_specs=[smem()] + [vmem()] * (1 + n_row),
            out_specs=[vmem()] * (n_col if last else 1),
            scratch_shapes=[
                pltpu.VMEM((sum(caps_in), rows, blk), jnp.bfloat16),
                pltpu.VMEM((n_col * cap + 1, rows, blk), jnp.float32),
            ],
            compiler_params=params,
            cost_estimate=pl.CostEstimate(flops=HIDE, bytes_accessed=COST, transcendentals=0),
            name="product",
        )(places, stored, *panels)
        later, _ = lax.optimization_barrier((heard, sums))
        packed += pack(spans[p + 2 : p + 3], later)
        if last:
            sums = [sums[0]] + [
                lax.ppermute(sums[i], "col", pairs(n_col, t))
                for i, t in enumerate(turns(n_col))
                if i > 0
            ]
        else:
            sums = [lax.all_to_all(sums[0], "col", 0, 0, tiled=True)]
        if result is not None and not last:
            places, result = lax.optimization_barrier((places, result))
        extra = [] if result is None else [result]
        result = pl.pallas_call(
            lambda *refs, first=first, n=len(sums): combine_kernel(n_col, n, blk, first, chunks, *refs),
            out_shape=jax.ShapeDtypeStruct(s_slab.shape, s_slab.dtype),
            in_specs=[smem()] + [vmem()] * (1 + len(sums)) + [anywhere()] * len(extra),
            out_specs=anywhere(),
            scratch_shapes=[
                pltpu.VMEM((pieces, rows, blk), jnp.float32),
                pltpu.VMEM((rows, width), jnp.bfloat16),
                pltpu.SemaphoreType.DMA((chunks,)),
            ],
            input_output_aliases={2 + len(sums): 0} if extra else {},
            compiler_params=params,
            cost_estimate=cost,
            name="combine",
        )(lists, s_slab, *sums, *extra)
    return result


def body(s_slab, p_blocks, p_index):
    blk = s_slab.shape[0]
    per_piece = s_slab.shape[1] // blk
    n_row = lax.axis_size("row")
    n_col = lax.axis_size("col")
    slots = p_blocks.shape[2]
    stored = p_blocks[0, 0]
    full = min(per_piece, slots)
    wide = -(-(2 + full) // 128) * 128
    parts = PARTS if sum(PARTS) == blk else (blk,)
    levels = [level for level in LEVELS if max(level) < full]
    levels.append((full, full, full))

    line, places = pl.pallas_call(
        lambda *refs: ask_kernel(n_row, n_col, per_piece, levels[:-1], *refs),
        out_shape=[
            jax.ShapeDtypeStruct((n_row * n_col, wide), jnp.int32),
            jax.ShapeDtypeStruct((6, slots), jnp.int32),
        ],
        name="ask",
    )(p_index)
    heard = lax.all_to_all(line, ("row", "col"), 0, 0, tiled=True)
    lines = heard.reshape(n_row * n_col, 1, wide)
    lists = heard.reshape(n_row, n_col, wide)[lax.axis_index("row")]

    def run(level):
        near, far, cap = level
        caps_in = [near, near] + [far] * (n_row - 2)
        return lambda: exchange(lines, lists, places, s_slab, stored, caps_in, cap, parts)

    if len(levels) == 1:
        return run(levels[0])()
    return lax.switch(jnp.max(heard[:, wide - 1]), [run(level) for level in levels])


def solution(mesh):
    placed = (
        P(None, ("row", "col")),
        P("row", "col", None, None, None),
        P("row", "col", None, None),
    )
    return jax.shard_map(
        body, mesh=mesh, in_specs=placed, out_specs=P(None, ("row", "col")), check_vma=False
    )
```

```python
import jax
import jax.numpy as jnp
from jax import lax
from jax.experimental import pallas as pl
from jax.experimental.pallas import tpu as pltpu
from jax.sharding import PartitionSpec as P

LEVELS = ((24, 17, 12), (24, 18, 13), (24, 19, 14), (26, 21, 15), (32, 25, 18))
PARTS = (32, 48, 48)
SHIFT = 1024
WINDOW = 5
COST = 1 << 16
HIDE = 30_000_000_000


def smem():
    return pl.BlockSpec(memory_space=pltpu.SMEM)


def anywhere():
    return pl.BlockSpec(memory_space=pl.ANY)


def vmem():
    return pl.BlockSpec(memory_space=pltpu.VMEM)


def pairs(n, t):
    return [(i, i ^ t) for i in range(n)]


def turns(n):
    return [t for t in range(n) if t < 3] + [t for t in range(n - 1, 2, -1)]


def number(index, per_piece, owner_of, n_owner, wide):
    slots = index.shape[1]
    f32 = jnp.float32
    lane = lax.broadcasted_iota(jnp.int32, (slots, slots), 1)
    sub = lax.broadcasted_iota(jnp.int32, (slots, slots), 0)
    key_r = index.astype(f32)
    key_c = jnp.sum(jnp.where(lane == sub, key_r, 0.0), axis=1, keepdims=True)
    index_c = jnp.maximum(key_c.astype(jnp.int32), 0)
    owner_r = owner_of(jnp.maximum(index, 0)).astype(f32)
    owner_c = owner_of(index_c).astype(f32)
    local_c = lax.rem(index_c, per_piece).astype(f32)
    same = jnp.where(key_c == key_r, 1.0, 0.0)
    before = jnp.where(lane < sub, 1.0, 0.0)
    after = jnp.where(sub < lane, 1.0, 0.0)
    kin = jnp.where(owner_c == owner_r, 1.0, 0.0)
    first_c = jnp.where(jnp.sum(same * before, axis=1, keepdims=True) == 0.0, 1.0, 0.0)
    first_c = jnp.where(key_c >= 0.0, first_c, 0.0)
    first_r = jnp.where(jnp.sum(same * after, axis=0, keepdims=True) == 0.0, 1.0, 0.0)
    first_r = jnp.where(key_r >= 0.0, first_r, 0.0)
    rank_c = jnp.sum(kin * before * first_r, axis=1, keepdims=True)
    rank_r = jnp.sum(same * (first_c * rank_c), axis=0, keepdims=True)
    lanes = lax.broadcasted_iota(jnp.int32, (slots, wide), 1).astype(f32)
    spot = jnp.where(lanes == rank_c + 1.0, local_c, 0.0) + jnp.where(lanes == 0.0, 1.0, 0.0)
    rows = []
    for owner in range(n_owner):
        mine = first_c * jnp.where(owner_c == float(owner), 1.0, 0.0)
        rows.append(jnp.sum(spot * mine, axis=0, keepdims=True))
    return owner_r.astype(jnp.int32), rank_r.astype(jnp.int32), first_r, rows


def ask_kernel(n_row, n_col, per_piece, levels, index, line, places):
    wide = line.shape[1]
    k, j = index[0, 0, 0:1, :], index[0, 0, 1:2, :]
    from_r, from_rank, _, asks = number(
        k, per_piece, lambda v: lax.div(v, per_piece * n_col), n_row, wide
    )
    to_r, to_rank, first, lists = number(
        j, per_piece, lambda v: lax.rem(lax.div(v, per_piece), n_col), n_col, wide
    )
    row = lax.axis_index("row")
    need = jnp.zeros((1, 1), jnp.float32)
    for near, far, col in levels:
        over = jnp.zeros((1, 1), jnp.float32)
        for owner, ask in enumerate(asks):
            cap = jnp.where((owner ^ row) <= 1, float(near), float(far))
            over = jnp.maximum(over, jnp.where(ask[:, 0:1] > cap, 1.0, 0.0))
        for item in lists:
            over = jnp.maximum(over, jnp.where(item[:, 0:1] > float(col), 1.0, 0.0))
        need = need + over
    lane = lax.broadcasted_iota(jnp.int32, (1, wide), 1)
    told = jnp.concatenate(lists, axis=0) * float(SHIFT)
    for owner, ask in enumerate(asks):
        values = jnp.where(lane == wide - 1, need, ask + told)
        line[owner * n_col : (owner + 1) * n_col, :] = values.astype(jnp.int32)
    alive = jnp.where(j >= 0, 1.0, 0.0)
    live = jnp.sum(alive, axis=1, keepdims=True)
    places[0:1, :] = from_r ^ row
    places[1:2, :] = from_rank
    places[2:3, :] = to_r
    places[3:4, :] = to_rank
    places[4:5, :] = first.astype(jnp.int32)
    places[5:6, :] = jnp.broadcast_to(live, j.shape).astype(jnp.int32)


def fetch(copies):
    for copy in copies:
        copy.start()
    for copy in copies:
        copy.wait()


def pack_kernel(n_row, n_col, blk, spans, heard, slab, *refs):
    packs, (asks, held, sems) = refs[: n_row * len(spans)], refs[n_row * len(spans) :]
    row, col = lax.axis_index("row"), lax.axis_index("col")
    start = spans[0][0]
    fetch(
        [
            pltpu.make_async_copy(heard.at[(row ^ t) * n_col + col], asks.at[t], sems.at[t])
            for t in range(n_row)
        ]
        + [pltpu.make_async_copy(slab.at[pl.ds(start, held.shape[0])], held, sems.at[n_row])]
    )
    for p, (first, rows) in enumerate(spans):
        for t in range(n_row):
            pack = packs[p * n_row + t]

            def copy(i, carry):
                at = pl.multiple_of((asks[t, 0, 1 + i] & (SHIFT - 1)) * blk, blk)
                pack[i] = held[first - start : first - start + rows, pl.ds(at, blk)]
                return carry

            lax.fori_loop(0, asks[t, 0, 0] & (SHIFT - 1), copy, 0)


def product_kernel(n_row, n_col, cap, base, group, places, stored, *refs):
    panels, sums, (held, total) = refs[:n_row], refs[n_row:-2], refs[-2:]
    turn = lax.axis_index("col") if len(sums) > 1 else 0
    for t, panel in enumerate(panels):
        held[base[t] : base[t] + panel.shape[0]] = panel[...]
    live = places[5, 0]

    def start(t):
        at = jnp.int32(base[0])
        for i in range(1, n_row):
            at = jnp.where(t == i, base[i], at)
        return at

    def step(g, carry):
        products = []
        for u in range(group):
            s = g * group + u
            here = start(places[0, s]) + places[1, s]
            products.append(jnp.dot(held[here], stored[s], preferred_element_type=jnp.float32))
        for u in range(group):
            s = g * group + u
            o = jnp.where(s < live, (places[2, s] ^ turn) * cap + places[3, s], n_col * cap)
            total[o] = jnp.where(places[4, s] == 1, 0.0, total[o]) + products[u]
        return carry

    lax.fori_loop(0, lax.div(live + group - 1, group), step, 0)
    for t in range(n_col):
        values = total[t * cap : (t + 1) * cap].astype(jnp.bfloat16)
        if len(sums) > 1:
            sums[turns(n_col).index(t)][...] = values
        else:
            sums[0][t] = values


def combine_kernel(n_col, n_sums, blk, first, chunks, lists, slab, *refs):
    sums, (out, total, ready, sems) = refs[:n_sums], refs[-4:]
    turn = lax.axis_index("col") if n_sums > 1 else 0
    pieces, rows = total.shape[:2]
    for i in range(pieces):
        total[i] = 3.0 * slab[first : first + rows, i * blk : (i + 1) * blk].astype(jnp.float32)
    for t in range(n_col):
        source = turns(n_col)[t] ^ turn if n_sums > 1 else t
        here = sums[t] if n_sums > 1 else sums[0].at[t]

        def add(i, carry):
            total[lists[source, 1 + i] >> 10] -= 2.0 * here[i].astype(jnp.float32)
            return carry

        lax.fori_loop(0, lists[source, 0] >> 10, add, 0)
    each = pieces // chunks
    copies = []
    for q in range(chunks):
        for i in range(q * each, (q + 1) * each):
            ready[:, i * blk : (i + 1) * blk] = total[i].astype(ready.dtype)
        here = pl.ds(q * each * blk, each * blk)
        copies.append(
            pltpu.make_async_copy(ready.at[:, here], out.at[pl.ds(first, rows), here], sems.at[q])
        )
        copies[-1].start()
    for copy in copies:
        copy.wait()


def exchange(heard, lists, places, s_slab, stored, caps_in, cap, parts):
    blk = s_slab.shape[0]
    width = s_slab.shape[1]
    n_row = lax.axis_size("row")
    n_col = lax.axis_size("col")
    slots = stored.shape[0]
    pieces = width // blk
    group = 8 if slots % 8 == 0 else 1
    chunks = 4 if pieces % 4 == 0 else 1
    base = [sum(caps_in[:t]) for t in range(n_row)]
    tight = sum(caps_in) <= 2 * slots
    params = pltpu.CompilerParams(vmem_limit_bytes=(16 if tight else 48) * 1024 * 1024)
    cost = pl.CostEstimate(flops=0, bytes_accessed=COST, transcendentals=0)
    spans = [(sum(parts[:i]), rows) for i, rows in enumerate(parts)]

    def pack(some, heard):
        if not some:
            return []
        done = pl.pallas_call(
            lambda *refs: pack_kernel(n_row, n_col, blk, some, *refs),
            out_shape=[
                jax.ShapeDtypeStruct((c, rows, blk), jnp.bfloat16)
                for first, rows in some
                for c in caps_in
            ],
            in_specs=[anywhere(), anywhere()],
            out_specs=[vmem()] * (n_row * len(some)),
            scratch_shapes=[
                pltpu.SMEM((n_row,) + heard.shape[1:], jnp.int32),
                pltpu.VMEM((sum(rows for first, rows in some), width), jnp.bfloat16),
                pltpu.SemaphoreType.DMA((n_row + 1,)),
            ],
            compiler_params=params,
            cost_estimate=cost,
            name="pack",
        )(heard, s_slab)
        return [done[i * n_row : (i + 1) * n_row] for i in range(len(some))]

    packed = pack(spans[:1], heard) + pack(spans[1:2], heard)
    if len(spans) > 1:
        places, packed[1] = lax.optimization_barrier((places, packed[1]))
    result = None
    for p, (first, rows) in enumerate(spans):
        packs = packed[p]
        last = len(spans) > 1 and first + rows == blk
        panels = [packs[0]] + [
            lax.ppermute(packs[t], "row", pairs(n_row, t)) for t in range(1, n_row)
        ]
        sums = pl.pallas_call(
            lambda *refs: product_kernel(n_row, n_col, cap, base, group, *refs),
            out_shape=[jax.ShapeDtypeStruct((cap, rows, blk), jnp.bfloat16)] * n_col
            if last
            else [jax.ShapeDtypeStruct((n_col, cap, rows, blk), jnp.bfloat16)],
            in_specs=[smem()] + [vmem()] * (1 + n_row),
            out_specs=[vmem()] * (n_col if last else 1),
            scratch_shapes=[
                pltpu.VMEM((sum(caps_in), rows, blk), jnp.bfloat16),
                pltpu.VMEM((n_col * cap + 1, rows, blk), jnp.float32),
            ],
            compiler_params=params,
            cost_estimate=pl.CostEstimate(flops=HIDE, bytes_accessed=COST, transcendentals=0),
            name="product",
        )(places, stored, *panels)
        later, _ = lax.optimization_barrier((heard, sums))
        packed += pack(spans[p + 2 : p + 3], later)
        if last:
            moved = [sums[0]]
            for i, t in enumerate(turns(n_col)[1:], 1):
                block = sums[i]
                if i > WINDOW:
                    block, _ = lax.optimization_barrier((block, moved[i - WINDOW]))
                moved.append(lax.ppermute(block, "col", pairs(n_col, t)))
            sums = moved
        else:
            sums = [lax.all_to_all(sums[0], "col", 0, 0, tiled=True)]
        if result is not None and not last:
            places, result = lax.optimization_barrier((places, result))
        extra = [] if result is None else [result]
        result = pl.pallas_call(
            lambda *refs, first=first, n=len(sums): combine_kernel(n_col, n, blk, first, chunks, *refs),
            out_shape=jax.ShapeDtypeStruct(s_slab.shape, s_slab.dtype),
            in_specs=[smem()] + [vmem()] * (1 + len(sums)) + [anywhere()] * len(extra),
            out_specs=anywhere(),
            scratch_shapes=[
                pltpu.VMEM((pieces, rows, blk), jnp.float32),
                pltpu.VMEM((rows, width), jnp.bfloat16),
                pltpu.SemaphoreType.DMA((chunks,)),
            ],
            input_output_aliases={2 + len(sums): 0} if extra else {},
            compiler_params=params,
            cost_estimate=cost,
            name="combine",
        )(lists, s_slab, *sums, *extra)
    return result


def body(s_slab, p_blocks, p_index):
    blk = s_slab.shape[0]
    per_piece = s_slab.shape[1] // blk
    n_row = lax.axis_size("row")
    n_col = lax.axis_size("col")
    slots = p_blocks.shape[2]
    stored = p_blocks[0, 0]
    full = min(per_piece, slots)
    wide = -(-(2 + full) // 128) * 128
    parts = PARTS if sum(PARTS) == blk else (blk,)
    levels = [level for level in LEVELS if max(level) < full]
    levels.append((full, full, full))

    line, places = pl.pallas_call(
        lambda *refs: ask_kernel(n_row, n_col, per_piece, levels[:-1], *refs),
        out_shape=[
            jax.ShapeDtypeStruct((n_row * n_col, wide), jnp.int32),
            jax.ShapeDtypeStruct((6, slots), jnp.int32),
        ],
        name="ask",
    )(p_index)
    heard = lax.all_to_all(line, ("row", "col"), 0, 0, tiled=True)
    lines = heard.reshape(n_row * n_col, 1, wide)
    lists = heard.reshape(n_row, n_col, wide)[lax.axis_index("row")]

    def run(level):
        near, far, cap = level
        caps_in = [near, near] + [far] * (n_row - 2)
        return lambda: exchange(lines, lists, places, s_slab, stored, caps_in, cap, parts)

    if len(levels) == 1:
        return run(levels[0])()
    return lax.switch(jnp.max(heard[:, wide - 1]), [run(level) for level in levels])


def solution(mesh):
    placed = (
        P(None, ("row", "col")),
        P("row", "col", None, None, None),
        P("row", "col", None, None),
    )
    return jax.shard_map(
        body, mesh=mesh, in_specs=placed, out_specs=P(None, ("row", "col")), check_vma=False
    )
```
